512 devices in a mesh: rep: 32 (over z_lo, x, core), dom: 16 (over y, z_hi).
Axes of the slice: x: 4, y: 8, z: 8 (z_hi: 2, z_lo: 4; z = z_hi * 4 + z_lo), core: 2. Of those that a mesh axis runs over, the one named last changes fastest.
Arguments:
- particle_locations: float32 [32, 3, 2048], P('rep', None, 'dom'), may hold values from 0 to 56, as said below
- particle_speeds: float32 [32, 3, 2048], P('rep', None, 'dom'), may hold values from -6 to 6
- acting_pulls: float32 [32, 3, 2048], P('rep', None, 'dom'), may hold values from -6 to 6
- reciprocal_particle_inertia: float32 [2048], P('dom'), may hold values from 0.25 to 2.5
- particle_elements: int32 [2048], P('dom'), may hold values from 0 to 88
- domain_real_particles: int32 [32, 16], P('rep', 'dom'), may hold values from 64 to 128, as said below
- halo_send_places: int32 [32, 2, 1024], P('rep', None, 'dom'), may hold values from 0 to 127, as said below
- adjacency_places: int32 [32, 16, 2048], P('rep', None, 'dom'), may hold values from 0 to 255, as said below
- filled_adjacency_places: int32 [32, 2048], P('rep', 'dom'), may hold values from 8 to 16
- exchange_target: int32 [32], P('rep'), may hold values from 0 to 31, as said below
- thermal_levels: float32 [32], replicated, may hold values from 300 to 600
- element_features: bfloat16 [89, 128], replicated, may hold values from -6 to 6
- first_distance_expansion: bfloat16 [8, 64], replicated, may hold values from -2 to 2
- first_distance_filter: bfloat16 [64, 256], replicated, may hold values from -0.75 to 0.75
- first_source_projection: bfloat16 [128, 128], replicated, may hold values from -0.5 to 0.5
- first_invariant_blend: bfloat16 [256, 128], replicated, may hold values from -0.375 to 0.375
- first_directional_change: bfloat16 [128, 128], replicated, may hold values from -0.5 to 0.5
- first_linear_potential_head: bfloat16 [128], replicated, may hold values from -0.5 to 0.5
- second_distance_expansion: bfloat16 [8, 64], replicated, may hold values from -2 to 2
- second_distance_filter: bfloat16 [64, 256], replicated, may hold values from -0.75 to 0.75
- second_source_projection: bfloat16 [128, 128], replicated, may hold values from -0.5 to 0.5
- second_invariant_blend: bfloat16 [128, 128], replicated, may hold values from -0.5 to 0.5
- final_head_intermediate: bfloat16 [128, 16], replicated, may hold values from -0.5 to 0.5
- final_head_projection: bfloat16 [16], replicated, may hold values from -1.5 to 1.5
Outputs:
- new_positions: float32 [32, 3, 2048], P('rep', None, 'dom')
- new_velocities: float32 [32, 3, 2048], P('rep', None, 'dom')
- new_forces: float32 [32, 3, 2048], P('rep', None, 'dom')
- domain_energy: float32 [32, 16], P('rep', 'dom')
The draws below stay inside these ranges and needn't reach their ends.
Inputs may be any that keep to these rules, and one draw needn't show every extreme that they name: `domain_real_particles`: each domain has at least 64 live atoms; in every replica some domain is full. `halo_send_places`: each row of a domain lists 64 distinct live slots of that domain, numbered within the domain. `adjacency_places`: entries below 128 are live own slots other than the atom itself; entries from 128 on are ghost positions of the extended array. exchange_target[r] is r, r - 1 or r + 1, and exchange_target[exchange_target[r]] = r. `particle_locations`: atoms of domain d have first coordinate in [3.5 d, 3.5 (d + 1)); the other two lie in [0, 5).
All inputs are finite; a program needn't handle non-finite values.
Results may differ from the reference program's by a relative error of at most 0.00105.
The reference program's roundings to bfloat16 on the way (of `kept`) count: a program that leaves them out, or rounds other values in their place, can miss the bound.
Values may be sent and summed in bfloat16 or wider, within the bound.
A program may use at most 128 MiB of HBM per device.

```python
import math
import jax
import jax.numpy as jnp
import numpy as np
from jax import lax

CHANNELS = 128
BASIS = 8
RADIAL = 64
READOUT = 16
SPECIES = 89
ATOMS_DEV = 128
GHOSTS = 64
NEIGHBOURS = 16
EVALS = 2
THERMAL_COPIES = 32
DOMAINS = 16
ATOMS = 2048


SLAB_WIDTH = 3.5


SIDE_LENGTH = 5.0


def shared_counts(key):
    spread = jax.random.randint(key, (THERMAL_COPIES, DOMAINS), ATOMS_DEV // 2, ATOMS_DEV + 1)
    fullest = jax.random.randint(jax.random.fold_in(key, 77), (THERMAL_COPIES, 1), 0, DOMAINS)
    return jnp.where(jnp.arange(DOMAINS)[None, :] == fullest, ATOMS_DEV, spread).astype(jnp.int32)


def draw_domain_real_particles(key, part):
    return shared_counts(key)


def draw_halo_send_places(key, part):
    counts = shared_counts(key)
    key = jax.random.fold_in(key, 1)
    slots = jnp.arange(ATOMS_DEV)
    scores = jax.random.randint(key, (THERMAL_COPIES, 2, DOMAINS, ATOMS_DEV), 0, 65536) * ATOMS_DEV + slots
    scores = scores + jnp.where(slots[None, None, None, :] >= counts[:, None, :, None], 2 ** 30, 0)
    order = jnp.argsort(scores, axis=-1)[..., :GHOSTS]
    return order.reshape(THERMAL_COPIES, 2, DOMAINS * GHOSTS).astype(jnp.int32)


def draw_adjacency_places(key, part):
    counts = shared_counts(key)
    key = jax.random.fold_in(key, 2)
    choose_key, ghost_key, own_key, top_key = jax.random.split(key, 4)
    shape = (THERMAL_COPIES, NEIGHBOURS, DOMAINS, ATOMS_DEV)
    from_ghost = jax.random.randint(choose_key, shape, 0, 2)
    ghost_pick = ATOMS_DEV + jax.random.randint(ghost_key, shape, 0, 2 * GHOSTS)
    limit = jnp.broadcast_to(counts[:, None, :, None], shape)
    own_pick = jax.random.randint(own_key, shape, 0, limit)
    atom = jnp.arange(ATOMS_DEV)
    own_pick = jnp.where(own_pick == atom, (own_pick + 1) % limit, own_pick)
    picks = jnp.where(from_ghost == 1, ghost_pick, own_pick)
    marked = jax.random.randint(top_key, (THERMAL_COPIES, 1, DOMAINS, 1), 0, ATOMS_DEV)
    first_slot = jnp.arange(NEIGHBOURS)[None, :, None, None] == 0
    picks = jnp.where(first_slot & (atom == marked), ATOMS_DEV + 2 * GHOSTS - 1, picks)
    return picks.reshape(THERMAL_COPIES, NEIGHBOURS, DOMAINS * ATOMS_DEV).astype(jnp.int32)


def draw_filled_adjacency_places(key, part):
    key = jax.random.fold_in(key, 3)
    count_key, mark_key = jax.random.split(key)
    counts = jax.random.randint(count_key, (THERMAL_COPIES, DOMAINS, ATOMS_DEV), NEIGHBOURS // 2, NEIGHBOURS + 1)
    marked = jax.random.randint(mark_key, (THERMAL_COPIES, DOMAINS, 1), 0, ATOMS_DEV)
    counts = jnp.where(jnp.arange(ATOMS_DEV) == marked, NEIGHBOURS, counts)
    return counts.reshape(THERMAL_COPIES, DOMAINS * ATOMS_DEV).astype(jnp.int32)


def draw_exchange_target(key, part):
    key = jax.random.fold_in(key, 4)
    parity_key, accept_key = jax.random.split(key)
    parity = jax.random.randint(parity_key, (), 0, 2).astype(jnp.int32)
    accepted = jax.random.randint(accept_key, (THERMAL_COPIES,), 0, 2).astype(jnp.int32)
    number = jnp.arange(THERMAL_COPIES).astype(jnp.int32)
    middle = THERMAL_COPIES // 2
    lower_member = ((number - parity) % 2 == 0) & (number + 1 < THERMAL_COPIES)
    touches_middle = (number == middle - 2) | (number == middle - 1) | (number == middle)
    bonds = (lower_member & ((accepted == 1) | touches_middle)).astype(jnp.int32)
    below = jnp.concatenate([jnp.zeros((1,), jnp.int32), bonds[:-1]])
    return jnp.where(bonds == 1, number + 1, jnp.where(below == 1, number - 1, number)).astype(jnp.int32)


def draw_particle_locations(key, part):
    key = jax.random.fold_in(key, 5)
    unit = jax.random.uniform(key, (THERMAL_COPIES, 3, ATOMS), jnp.float32)
    domain = (jnp.arange(ATOMS) // ATOMS_DEV).astype(jnp.float32)
    along = (domain[None, :] + unit[:, 0]) * SLAB_WIDTH
    return jnp.stack([along, unit[:, 1] * SIDE_LENGTH, unit[:, 2] * SIDE_LENGTH], 1).astype(jnp.float32)


def set_ends(array, key, least, largest):
    longest = array.shape.index(max(array.shape))
    spots = []
    for shift in (0, 1):
        where = [jax.random.randint(jax.random.fold_in(key, axis), (), 0, length) for axis, length in enumerate(array.shape)]
        where[longest] = (where[longest] + shift) % array.shape[longest]
        spots.append(tuple(where))
    return array.at[spots[0]].set(least).at[spots[1]].set(largest)


def level_of(stream_key, extent, cuts, least, high):
    def one(dim, shards_of):
        draws = jax.random.uniform(jax.random.fold_in(jax.random.fold_in(stream_key, 6), dim), (shards_of,), jnp.float32, least / len(cuts), high / len(cuts))
        return jnp.repeat(jnp.exp(draws), extent[dim] // shards_of).reshape((-1,) + (1,) * (len(extent) - dim - 1))

    factor_of = one(*cuts[0])
    for cut in cuts[1:]:
        factor_of = factor_of * one(*cut)
    return factor_of


def cumulative_ranks(number_of, slope):
    loads = [(1 << 20) // math.isqrt(rank ** slope) + 1 for rank in range(1, number_of + 1)]
    scale = 1 + sum(loads) // (1 << 30)
    return np.cumsum(np.array([max(1, weight // scale) for weight in loads]))


def skewed_ids(key, extent, amount, slope):
    table = cumulative_ranks(amount, slope)
    lot = jax.random.randint(jax.random.fold_in(key, 1), extent, 0, int(table[amount - 1]))
    rank = jnp.searchsorted(jnp.asarray(table, jnp.int32), lot, side="right")
    return jax.random.permutation(jax.random.fold_in(key, 2), amount)[rank].astype(jnp.int32)


def centred(rng, dims, deviation, most, shards=(), kind=jnp.bfloat16):
    level = level_of(rng, dims, shards, -0.22, 0.18) if shards else 1.0
    drawn = jax.random.normal(rng, dims, jnp.float32) * deviation * level
    return jnp.minimum(jnp.maximum(drawn, -most), most).astype(kind)


def setup_inputs(seed: int = 0) -> dict:
    key_list = jax.random.split(jax.random.key(seed), 25)
    particle_locations = draw_particle_locations(jax.random.fold_in(key_list[24], 71), 0)
    particle_speeds = centred(key_list[1], (THERMAL_COPIES, 3, ATOMS), 1.0, 6.0, ((0, 32), (2, 16)), jnp.float32)
    acting_pulls = centred(key_list[2], (THERMAL_COPIES, 3, ATOMS), 1.0, 6.0, ((0, 32), (2, 16)), jnp.float32)
    reciprocal_particle_inertia = jnp.clip(jnp.exp(math.log(2.5) - 2.3025851 * jax.random.uniform(key_list[3], (ATOMS,), jnp.float32) ** level_of(key_list[3], (ATOMS,), ((0, 16),), -0.2, 0.2)), 0.25, 2.5)
    particle_elements = set_ends(skewed_ids(key_list[4], (ATOMS,), SPECIES, 2), jax.random.fold_in(key_list[4], 3), 0, SPECIES - 1).astype(jnp.int32)
    domain_real_particles = draw_domain_real_particles(jax.random.fold_in(key_list[24], 71), 0)
    halo_send_places = draw_halo_send_places(jax.random.fold_in(key_list[24], 71), 0)
    adjacency_places = draw_adjacency_places(jax.random.fold_in(key_list[24], 71), 0)
    filled_adjacency_places = draw_filled_adjacency_places(jax.random.fold_in(key_list[24], 71), 0)
    exchange_target = draw_exchange_target(jax.random.fold_in(key_list[24], 71), 0)
    thermal_levels = jnp.clip(jnp.exp(jax.random.uniform(key_list[10], (THERMAL_COPIES,), jnp.float32, math.log(300.0), math.log(600.0))), 300.0, 600.0)
    element_features = centred(key_list[11], (SPECIES, CHANNELS), 1.0, 6.0)
    first_distance_expansion = centred(key_list[12], (BASIS, RADIAL), BASIS ** -0.5, 2.0)
    first_distance_filter = centred(key_list[13], (RADIAL, 2 * CHANNELS), RADIAL ** -0.5, 0.75)
    first_source_projection = centred(key_list[14], (CHANNELS, CHANNELS), CHANNELS ** -0.5, 0.5)
    first_invariant_blend = centred(key_list[15], (2 * CHANNELS, CHANNELS), (2 * CHANNELS) ** -0.5, 0.375)
    first_directional_change = centred(key_list[16], (CHANNELS, CHANNELS), CHANNELS ** -0.5, 0.5)
    first_linear_potential_head = centred(key_list[17], (CHANNELS,), CHANNELS ** -0.5, 0.5)
    second_distance_expansion = centred(key_list[18], (BASIS, RADIAL), BASIS ** -0.5, 2.0)
    second_distance_filter = centred(key_list[19], (RADIAL, 2 * CHANNELS), RADIAL ** -0.5, 0.75)
    second_source_projection = centred(key_list[20], (CHANNELS, CHANNELS), CHANNELS ** -0.5, 0.5)
    second_invariant_blend = centred(key_list[21], (CHANNELS, CHANNELS), CHANNELS ** -0.5, 0.5)
    final_head_intermediate = centred(key_list[22], (CHANNELS, READOUT), CHANNELS ** -0.5, 0.5)
    final_head_projection = centred(key_list[23], (READOUT,), READOUT ** -0.5, 1.5)
    return {"particle_locations": particle_locations, "particle_speeds": particle_speeds, "acting_pulls": acting_pulls, "reciprocal_particle_inertia": reciprocal_particle_inertia, "particle_elements": particle_elements, "domain_real_particles": domain_real_particles, "halo_send_places": halo_send_places, "adjacency_places": adjacency_places, "filled_adjacency_places": filled_adjacency_places, "exchange_target": exchange_target, "thermal_levels": thermal_levels, "element_features": element_features, "first_distance_expansion": first_distance_expansion, "first_distance_filter": first_distance_filter, "first_source_projection": first_source_projection, "first_invariant_blend": first_invariant_blend, "first_directional_change": first_directional_change, "first_linear_potential_head": first_linear_potential_head, "second_distance_expansion": second_distance_expansion, "second_distance_filter": second_distance_filter, "second_source_projection": second_source_projection, "second_invariant_blend": second_invariant_blend, "final_head_intermediate": final_head_intermediate, "final_head_projection": final_head_projection}


precise = lax.Precision.HIGHEST
CUTOFF = 6.0
SOFTEN = 0.25
SLAB_WIDTH = 3.5
timestep = 0.4

def geometry(own_coords, ext_coords, nearby):
    across = jnp.take(ext_coords, nearby, axis=1) - own_coords[:, None, :]
    distance = jnp.sqrt(lax.optimization_barrier(jnp.sum(across * across, axis=0)) + SOFTEN)
    return (across / distance[None], distance)

def radial_weights(distance, basis_w, output_w, valid):
    scaled = jnp.minimum(distance / CUTOFF, 1.0)
    envelope = 1.0 - 21.0 * scaled ** 5 + 35.0 * scaled ** 6 - 15.0 * scaled ** 7
    orders = jnp.arange(1, basis_w.shape[0] + 1).astype(jnp.float32)
    bessel = jnp.sqrt(2.0 / CUTOFF) * jnp.sin(orders[:, None, None] * jnp.pi * distance[None] / CUTOFF) / distance[None] * envelope[None]
    hidden = jax.nn.silu(jnp.einsum('nr,nka->rka', basis_w.astype(jnp.float32), bessel, precision=precise))
    return jnp.einsum('rc,rka->cka', output_w.astype(jnp.float32), hidden, precision=precise) * valid[None]

def first_layer(own_coords, ext_coords, ext_species, nearby, valid, element_features, first_distance_expansion, first_distance_filter, first_source_projection, first_invariant_blend, first_directional_change, first_linear_potential_head):
    table = element_features.astype(jnp.float32).T
    initial = jnp.take(table, ext_species, axis=1)
    lifted = jnp.dot(first_source_projection.astype(jnp.float32).T, initial, precision=precise)
    direction, distance = geometry(own_coords, ext_coords, nearby)
    radial = radial_weights(distance, first_distance_expansion, first_distance_filter, valid)
    channels = initial.shape[0]
    count = nearby.shape[0]
    atoms = own_coords.shape[1]
    sender = jnp.take(lifted, nearby, axis=1)
    invariant = lax.optimization_barrier(jnp.sum(radial[:channels] * sender, axis=1)) / count
    vectors = jnp.einsum('mka,cka->mca', direction, radial[channels:] * sender, precision=precise) / count
    squares = lax.optimization_barrier(jnp.sum(vectors * vectors, axis=0))
    scalars = initial[:, :atoms] + jnp.dot(first_invariant_blend.astype(jnp.float32).T, jnp.concatenate([invariant, squares], 0), precision=precise)
    vector_out = jnp.einsum('cd,mca->mda', first_directional_change.astype(jnp.float32), vectors, precision=precise)
    energy = jnp.dot(first_linear_potential_head.astype(jnp.float32), scalars, precision=precise)
    return (jnp.concatenate([scalars, vector_out.reshape(3 * channels, atoms)], 0), energy)

def second_layer(own_coords, ext_coords, ext_features, nearby, valid, second_distance_expansion, second_distance_filter, second_source_projection, second_invariant_blend, final_head_intermediate, final_head_projection):
    channels = second_source_projection.shape[0]
    total = ext_features.shape[1]
    lifting = second_source_projection.astype(jnp.float32)
    scalars = jnp.dot(lifting.T, ext_features[:channels], precision=precise)
    vectors = jnp.einsum('cd,mce->mde', lifting, ext_features[channels:].reshape(3, channels, total), precision=precise)
    direction, distance = geometry(own_coords, ext_coords, nearby)
    radial = radial_weights(distance, second_distance_expansion, second_distance_filter, valid)
    count = nearby.shape[0]
    atoms = own_coords.shape[1]
    near_scalar = jnp.take(scalars, nearby, axis=1)
    near_vector = jnp.take(vectors, nearby, axis=2)
    along = lax.optimization_barrier(jnp.sum(direction[:, None] * near_vector, axis=0))
    message = lax.optimization_barrier(jnp.sum(radial[:channels] * near_scalar + radial[channels:] * along, axis=1)) / count
    mixed = ext_features[:channels, :atoms] + jnp.dot(second_invariant_blend.astype(jnp.float32).T, message, precision=precise)
    hidden = jax.nn.silu(jnp.dot(final_head_intermediate.astype(jnp.float32).T, mixed, precision=precise))
    return jnp.dot(final_head_projection.astype(jnp.float32), hidden, precision=precise)

def rounded(values):
    stored = lax.optimization_barrier(values.astype(jnp.bfloat16))
    return values + lax.stop_gradient(stored.astype(jnp.float32) - values)

def replica_energy(particle_elements, counts, ghost_rows, nearby_all, nearby_count, first_params, second_params):
    domains = counts.shape[0]
    atoms = particle_elements.shape[0] // domains
    ghosts = ghost_rows.shape[1] // domains
    box = SLAB_WIDTH * domains
    domain_ids = jnp.arange(domains).astype(jnp.int32)
    slots = jnp.arange(atoms).astype(jnp.int32)

    def extended(domain):
        lower = (domain - 1) % domains
        upper = (domain + 1) % domains
        own = domain * atoms + slots
        from_lower = lower * atoms + lax.dynamic_slice_in_dim(ghost_rows[1], (lower * ghosts).astype(jnp.int32), ghosts)
        from_upper = upper * atoms + lax.dynamic_slice_in_dim(ghost_rows[0], (upper * ghosts).astype(jnp.int32), ghosts)
        index = jnp.concatenate([own, from_lower, from_upper]).astype(jnp.int32)
        lower_shift = jnp.where(domain == 0, -box, 0.0)
        upper_shift = jnp.where(domain == domains - 1, box, 0.0)
        shift = jnp.concatenate([jnp.zeros((atoms,), jnp.float32), jnp.full((ghosts,), lower_shift, jnp.float32), jnp.full((ghosts,), upper_shift, jnp.float32)])
        return (index, shift)

    def masks(domain):
        live_bool = slots < counts[domain]
        nearby = lax.dynamic_slice_in_dim(nearby_all, (domain * atoms).astype(jnp.int32), atoms, 1)
        used = lax.dynamic_slice_in_dim(nearby_count, (domain * atoms).astype(jnp.int32), atoms)
        valid = ((jnp.arange(nearby.shape[0])[:, None] < used[None, :]) & live_bool[None, :]).astype(jnp.float32)
        return (nearby, valid)

    def ext_coords(coords, domain):
        index, shift = extended(domain)
        gathered = jnp.take(coords, index, axis=1)
        zeros = jnp.zeros_like(shift)
        return (gathered + jnp.stack([shift, zeros, zeros]), index)

    def energy(coords):

        def first(domain):
            ext, index = ext_coords(coords, domain)
            nearby, valid = masks(domain)
            return first_layer(ext[:, :atoms], ext, jnp.take(particle_elements, index), nearby, valid, *first_params)
        features, first_energy = lax.map(first, domain_ids)
        kept = rounded(features)
        width = kept.shape[1]
        flat = jnp.transpose(kept, (1, 0, 2)).reshape(width, domains * atoms)

        def second(domain):
            ext, index = ext_coords(coords, domain)
            nearby, valid = masks(domain)
            return second_layer(ext[:, :atoms], ext, jnp.take(flat, index, axis=1), nearby, valid, *second_params)
        second_energy = lax.map(second, domain_ids)
        live = (slots[None, :] < counts[:, None]).astype(jnp.float32)
        per_domain = lax.optimization_barrier(jnp.sum(live * (first_energy + second_energy), axis=1))
        return (jnp.sum(per_domain), per_domain)
    return energy

def reference(particle_locations, particle_speeds, acting_pulls, reciprocal_particle_inertia, particle_elements, domain_real_particles, halo_send_places, adjacency_places, filled_adjacency_places, exchange_target, thermal_levels, element_features, first_distance_expansion, first_distance_filter, first_source_projection, first_invariant_blend, first_directional_change, first_linear_potential_head, second_distance_expansion, second_distance_filter, second_source_projection, second_invariant_blend, final_head_intermediate, final_head_projection):
    first_params = (element_features, first_distance_expansion, first_distance_filter, first_source_projection, first_invariant_blend, first_directional_change, first_linear_potential_head)
    second_params = (second_distance_expansion, second_distance_filter, second_source_projection, second_invariant_blend, final_head_intermediate, final_head_projection)

    def run(items):
        coords, velocity, force_now, counts, ghost_rows, nearby_all, nearby_count = items
        energy = replica_energy(particle_elements, counts, ghost_rows, nearby_all, nearby_count, first_params, second_params)
        per_domain = jnp.zeros(counts.shape, jnp.float32)
        for repeat in range(EVALS):
            halfway = velocity + 0.5 * timestep * force_now * reciprocal_particle_inertia
            coords = coords + timestep * halfway
            (total, per_domain), gradient = jax.value_and_grad(energy, has_aux=True)(coords)
            force_now = -gradient
            velocity = halfway + 0.5 * timestep * force_now * reciprocal_particle_inertia
        return (coords, velocity, force_now, per_domain)
    coords, velocity, force_now, per_domain = lax.map(run, (particle_locations, particle_speeds, acting_pulls, domain_real_particles, halo_send_places, adjacency_places, filled_adjacency_places))
    multiplier_amount = jnp.sqrt(thermal_levels / thermal_levels[exchange_target])
    return (coords[exchange_target], velocity[exchange_target] * multiplier_amount[:, None, None], force_now[exchange_target], per_domain[exchange_target])
```

```python
import math

import jax
import jax.numpy as jnp
from jax import lax
from jax.experimental import pallas as pl
from jax.experimental.pallas import tpu as pltpu
from jax.sharding import PartitionSpec as P

MESH = pl.DeviceIdType.MESH
F32 = jnp.float32
BF16 = jnp.bfloat16
I32 = jnp.int32

CUTOFF = 6.0
SOFTEN = 0.25
SLAB_WIDTH = 3.5
TIMESTEP = 0.4
EVALS = 2
C = 128
A = 128
K = 16
EDGES = 2 * K * A
OWN = K * A
CHUNK = 512
OFFSETS = (-2, -1, 1, 2)
SEGMENTS = ((0, 16), (16, 24), (24, 32))

SIN_TERMS = [(-1) ** j * math.pi ** (2 * j + 1) / math.factorial(2 * j + 1) for j in range(7)]
COS_TERMS = [(-1) ** j * math.pi ** (2 * j) / math.factorial(2 * j) for j in range(7)]


def dot(a, b):
    return jnp.dot(a, b, preferred_element_type=F32)


def dot_nt(a, b):
    return lax.dot_general(a, b, (((1,), (1,)), ((), ())), preferred_element_type=F32)


def halves(x):
    hi = x.astype(BF16)
    return hi, (x - hi.astype(F32)).astype(BF16)


def mm2(w, x):
    hi, lo = halves(x)
    return dot(w, hi) + dot(w, lo)


def thirds(x):
    hi = x.astype(BF16).astype(F32)
    rest = x - hi
    mid = rest.astype(BF16).astype(F32)
    return jnp.concatenate([hi, mid, rest - mid], 0).astype(BF16)


def joined(g):
    return g[0:8] + g[8:16] + g[16:24]


def polynomial(terms, z):
    total = jnp.full_like(z, terms[-1])
    for term in terms[-2::-1]:
        total = total * z + term
    return total


def lanes_below_64(shape):
    return lax.broadcasted_iota(I32, shape, 1) < 64


def lower_twice(x):
    return jnp.where(lanes_below_64(x.shape), x, pltpu.roll(x, 64, 1))


def upper_twice(x):
    return jnp.where(lanes_below_64(x.shape), pltpu.roll(x, 64, 1), x)


def octets(x):
    return jnp.sum(x.reshape(x.shape[0] // 8, 8, x.shape[1]), axis=0)


def sigmoid(x):
    return 0.5 * jnp.tanh(0.5 * x) + 0.5


def make_kernel(domains, replicas):
    box = SLAB_WIDTH * domains

    def kernel(
        pos_in, vel_in, frc_in, inertia_in, species_in, count_in, halo_in, adj_in, filled_in, target_in, levels_in,
        table_in, basis1_in, out1_in, source1_in, blend1_in, change1_in, head1_in,
        basis2_in, out2_in, source2_in, blend2_in, head2_in, proj2_in,
        pos_out, vel_out, frc_out, energy_out,
        pos, half, frc, adj, onehot, listhot, lift, h0, tabf,
        blend1_t, change1_t, source2_t, source2_s, blend2_t, head2_t, basis_t, basis_b, out1_t, out2_t,
        head1_col, proj2_col,
        unit, inverse, slope, sd1, sd2, r1, r2, sv, nodes, acc2, da2,
        dsv_hi, dsv_lo, dr1_hi, dr1_lo, dr2_hi, dr2_lo, du, dnodes, dacross, energy_row,
        a_out, a_in, s_out, s_in, b_out, b_in, c_out, c_in,
        a_send, a_recv, s_send, s_recv, b_send, b_recv, c_send, c_recv,
    ):
        dom = lax.axis_index("dom")
        rep = lax.axis_index("rep")
        around = [lax.rem(dom + off + domains, domains) for off in OFFSETS]
        rep_up, rep_down = lax.rem(rep + 1, replicas), lax.rem(rep + replicas - 1, replicas)

        def a_copies(it):
            return [
                pltpu.make_async_remote_copy(
                    src_ref=a_out.at[it], dst_ref=a_in.at[it, 3 - j],
                    send_sem=a_send.at[it, j], recv_sem=a_recv.at[it, 3 - j],
                    device_id=(rep, around[j]), device_id_type=MESH)
                for j in range(4)
            ]

        def b_copies(it):
            return [
                pltpu.make_async_remote_copy(
                    src_ref=b_out.at[it, j], dst_ref=b_in.at[it, 3 - j],
                    send_sem=b_send.at[it, j], recv_sem=b_recv.at[it, 3 - j],
                    device_id=(rep, around[j]), device_id_type=MESH)
                for j in range(4)
            ]

        def s_copies():
            return [
                pltpu.make_async_remote_copy(
                    src_ref=s_out, dst_ref=s_in.at[1 - j],
                    send_sem=s_send.at[j], recv_sem=s_recv.at[1 - j],
                    device_id=(rep, around[1 + j]), device_id_type=MESH)
                for j in range(2)
            ]

        def c_copies():
            return [
                pltpu.make_async_remote_copy(
                    src_ref=c_out, dst_ref=c_in.at[j],
                    send_sem=c_send.at[j], recv_sem=c_recv.at[j],
                    device_id=(to, dom), device_id_type=MESH)
                for j, to in ((0, rep_up), (1, rep_down))
            ]

        barrier = pltpu.get_barrier_semaphore()
        for j in range(4):
            pl.semaphore_signal(barrier, inc=1, device_id=(rep, around[j]), device_id_type=MESH)
        for to in (rep_up, rep_down):
            pl.semaphore_signal(barrier, inc=1, device_id=(to, dom), device_id_type=MESH)

        rows8 = lax.broadcasted_iota(I32, (8, A), 0)
        inertia = jnp.broadcast_to(inertia_in[...], (8, A))
        live_row = lax.broadcasted_iota(I32, (1, A), 1) < jnp.broadcast_to(count_in[...], (1, A))
        live = live_row.astype(F32)

        for ref, source in ((pos, pos_in), (half, vel_in), (frc, frc_in)):
            ref[...] = jnp.zeros((8, A), F32)
            ref[0:3, :] = source[0]
        pos[3:4, :] = species_in[...].astype(F32)

        numbers = lax.broadcasted_iota(I32, (A, A), 0)
        listed = jnp.concatenate([halo_in[0, 1:2, :], halo_in[0, 0:1, :]], axis=1)
        listhot[...] = (numbers == jnp.broadcast_to(listed, (A, A))).astype(F32).astype(BF16)

        def advance(it):
            halfway = half[...] + 0.5 * TIMESTEP * frc[...] * inertia
            half[...] = halfway
            moved = pos[...] + TIMESTEP * halfway
            pos[...] = moved
            a_out[it, :, 0:A] = moved
            a_out[it, :, A:2 * A] = joined(dot(thirds(moved), listhot[...]))

        advance(0)
        used = (lax.broadcasted_iota(I32, (K, A), 0) < jnp.broadcast_to(filled_in[...], (K, A))) & jnp.broadcast_to(
            live_row, (K, A))
        coded = jnp.where(used, adj_in[0] + 1, 0).astype(F32)
        adj[0:K, :] = coded
        s_out[...] = dot(coded.astype(BF16), listhot[...])

        pl.semaphore_wait(barrier, 6)
        for copy in a_copies(0) + s_copies():
            copy.start()

        blend1_t[...] = blend1_in[...].astype(F32).T.astype(BF16)
        change1_t[...] = change1_in[...].astype(F32).T.astype(BF16)
        scaled2 = source2_in[...].astype(F32) * (1.0 / K)
        source2_s[...] = scaled2.astype(BF16)
        source2_t[...] = scaled2.T.astype(BF16)
        blend2_t[...] = blend2_in[...].astype(F32).T.astype(BF16)
        head2_t[...] = head2_in[...].astype(F32).T.astype(BF16)
        both = jnp.concatenate([basis1_in[...].astype(F32), basis2_in[...].astype(F32)], axis=1)
        basis_b[...] = both.astype(BF16)
        both_t = jnp.concatenate([both, both], axis=0).T
        basis_t[...] = both_t.astype(BF16)
        for ref, source in ((out1_t, out1_in), (out2_t, out2_in)):
            whole = source[...].astype(F32)
            ref[...] = jnp.concatenate([whole, whole], axis=0).T.astype(BF16)
        head1_col[...] = jnp.broadcast_to(head1_in[...].astype(F32), (A, C)).T
        proj2_col[...] = jnp.broadcast_to(proj2_in[...].astype(F32), (A, 16)).T
        tabf[...] = jnp.zeros((C, C), F32)
        tabf[0:table_in.shape[0], :] = table_in[...].astype(F32)
        table_t = tabf[...].T.astype(BF16)
        source1_t = (source1_in[...].astype(F32) * (1.0 / K)).T.astype(BF16)

        ordinals = (lax.broadcasted_iota(I32, (2 * A, A), 0) + 1).astype(F32)

        def fill(b, carry):
            row = jnp.broadcast_to(adj[pl.ds(b, 1), :], (2 * A, A))
            onehot[:, pl.ds(pl.multiple_of(b * A, A), A)] = (ordinals == row).astype(F32).astype(BF16)
            return carry

        lax.fori_loop(0, K, fill, 0)

        for copy in s_copies():
            copy.wait()
        lower, upper = s_in[0], s_in[1]
        below = lanes_below_64((8, A))
        adj[K:K + 8, :] = jnp.where(below, lower[0:8], pltpu.roll(lower[8:16], 64, 1))
        adj[K + 8:K + 16, :] = jnp.where(below, pltpu.roll(upper[0:8], 64, 1), upper[8:16])
        lax.fori_loop(K, 2 * K, fill, 0)

        def shifts(number):
            down = jnp.where(number == 0, -box, 0.0).astype(F32)
            up = jnp.where(number == domains - 1, box, 0.0).astype(F32)
            return jnp.where(rows8 == 0, jnp.where(below, down, up), 0.0)

        own_shift, lower_shift, upper_shift = shifts(dom), shifts(around[1]), shifts(around[2])

        def extended(it):
            l2, l1, u1, u2 = [a_in[it, j] for j in range(4)]
            own = a_out[it]
            e0 = jnp.concatenate([own[:, :A], jnp.where(below, l1[:, A:], u1[:, A:]) + own_shift], axis=1)
            el = jnp.concatenate([l1[:, :A], jnp.where(below, l2[:, A:], own[:, A:]) + lower_shift], axis=1)
            eu = jnp.concatenate([u1[:, :A], jnp.where(below, own[:, A:], u2[:, A:]) + upper_shift], axis=1)
            centres = (own[:, :A], lower_twice(l1[:, A:]), upper_twice(u1[:, A:]))
            return (e0, el, eu), centres

        def chunk_of(i):
            return pl.ds(pl.multiple_of(i * CHUNK, CHUNK), CHUNK)

        per = CHUNK // A
        chunk_ranges = [(a // per, b // per) for a, b in SEGMENTS]

        def evaluate(it, carry):
            for copy in a_copies(it):
                copy.wait()
            exts, centres = extended(it)

            @pl.when(it == 0)
            def _():
                for s, ext in enumerate(exts):
                    kinds = jnp.broadcast_to(ext[3:4, :], (C, 2 * A))
                    which = lax.broadcasted_iota(I32, (C, 2 * A), 0).astype(F32)
                    initial = dot(table_t, (kinds == which).astype(F32).astype(BF16))
                    if s == 0:
                        h0[...] = initial
                    lifted = dot(source1_t, initial.astype(BF16))
                    hi, lo = halves(lifted)

                    def spread(i, c):
                        hot = onehot[:, chunk_of(i)]
                        lift[:, chunk_of(i)] = dot(hi, hot) + dot(lo, hot)
                        return c

                    lax.fori_loop(*chunk_ranges[s], spread, 0)

            wide8 = lax.broadcasted_iota(I32, (8, CHUNK), 0)
            order = (wide8 + 1).astype(F32)
            spatial = wide8 < 3

            for s, ext in enumerate(exts):
                pieces = thirds(ext)
                centre = jnp.concatenate([centres[s]] * per, axis=1)

                def radial(i, c):
                    here = chunk_of(i)
                    across = jnp.where(spatial, joined(dot(pieces, onehot[:, here])) - centre, 0.0)
                    squared = jnp.broadcast_to(jnp.sum(across * across, axis=0, keepdims=True), (8, CHUNK)) + SOFTEN
                    rd = lax.rsqrt(squared)
                    rd = rd * (1.5 - 0.5 * squared * rd * rd)
                    t = jnp.minimum(squared * rd * (1.0 / CUTOFF), 1.0)
                    y = order * t
                    turns = jnp.floor(y + 0.5)
                    r = y - turns
                    sign = 1.0 - 2.0 * (turns - 2.0 * jnp.floor(0.5 * turns))
                    z = r * r
                    sine = sign * r * polynomial(SIN_TERMS, z)
                    cosine = sign * polynomial(COS_TERMS, z)
                    t2 = t * t
                    t4 = t2 * t2
                    envelope = 1.0 + t4 * t * (-21.0 + t * (35.0 - 15.0 * t))
                    fall = -105.0 * t4 * (1.0 - t) * (1.0 - t)
                    front = math.sqrt(2.0 / CUTOFF) * rd
                    bessel = front * sine * envelope
                    unit[:, here] = across * rd
                    inverse[:, here] = rd
                    slope[:, here] = front * (
                        order * (math.pi / CUTOFF) * cosine * envelope
                        + sine * (fall * (1.0 / CUTOFF) - envelope * rd))
                    hi = bessel.astype(BF16).astype(F32)
                    stacked = jnp.concatenate([hi, bessel - hi], axis=0).astype(BF16)
                    pre = dot(basis_t[...] if s == 0 else basis_t[0:64, :], stacked)
                    sg = sigmoid(pre)
                    hidden = pre * sg
                    rise = sg + hidden * (1.0 - sg)
                    sd1[:, here] = rise[0:64]
                    hi, lo = halves(hidden)
                    r1[:, here] = dot(out1_t[...], jnp.concatenate([hi[0:64], lo[0:64]], axis=0))
                    if s == 0:
                        sd2[:, here] = rise[64:128]
                        r2[:, here] = dot(out2_t[...], jnp.concatenate([hi[64:128], lo[64:128]], axis=0))
                    return c

                lax.fori_loop(*chunk_ranges[s], radial, 0)

            def messages(cc, c):
                at = pl.multiple_of(cc * 32, 32)
                sums = []
                for first, last in SEGMENTS:
                    m = [jnp.zeros((32, A), F32) for _ in range(4)]
                    for b in range(first, last):
                        here = slice(b * A, (b + 1) * A)
                        sender = lift[pl.ds(at, 32), here]
                        m[0] = m[0] + r1[pl.ds(at, 32), here] * sender
                        through = r1[pl.ds(C + at, 32), here] * sender
                        for d in range(3):
                            m[1 + d] = m[1 + d] + unit[d:d + 1, here] * through
                    sums.append(m)
                for d in range(4):
                    row = pl.ds(d * C + at, 32)
                    nodes[row, 0:A] = sums[0][d]
                    lo, up = sums[1][d], sums[2][d]
                    lo = lo + pltpu.roll(lo, 64, 1)
                    up = up + pltpu.roll(up, 64, 1)
                    nodes[row, A:2 * A] = jnp.where(lanes_below_64((32, A)), lo, up)
                return c

            lax.fori_loop(0, C // 32, messages, 0)

            vectors = [nodes[(1 + d) * C:(2 + d) * C, :] for d in range(3)]
            squares = vectors[0] * vectors[0] + vectors[1] * vectors[1] + vectors[2] * vectors[2]
            scalars = h0[...] + mm2(blend1_t[...], jnp.concatenate([nodes[0:C, :], squares], axis=0))
            e1 = jnp.sum(head1_col[...] * scalars[:, 0:A], axis=0, keepdims=True)
            kept = [scalars.astype(BF16)] + [mm2(change1_t[...], v).astype(BF16) for v in vectors]
            projected = jnp.concatenate([dot(source2_t[...], f) for f in kept], axis=0)
            sv_hi, sv_lo = halves(projected)

            def gather2(i, c):
                hot = onehot[:, chunk_of(i)]
                sv[:, chunk_of(i)] = dot(sv_hi, hot) + dot(sv_lo, hot)
                return c

            lax.fori_loop(0, OWN // CHUNK, gather2, 0)

            def messages2(cc, c):
                at = pl.multiple_of(cc * 32, 32)
                total = jnp.zeros((32, A), F32)
                for b in range(K):
                    here = slice(b * A, (b + 1) * A)
                    along = unit[0:1, here] * sv[pl.ds(C + at, 32), here]
                    along = along + unit[1:2, here] * sv[pl.ds(2 * C + at, 32), here]
                    along = along + unit[2:3, here] * sv[pl.ds(3 * C + at, 32), here]
                    total = total + r2[pl.ds(at, 32), here] * sv[pl.ds(at, 32), here]
                    total = total + r2[pl.ds(C + at, 32), here] * along
                acc2[pl.ds(at, 32), :] = total
                return c

            lax.fori_loop(0, C // 32, messages2, 0)

            mixed = kept[0][:, 0:A].astype(F32) + mm2(blend2_t[...], acc2[...])
            pre = mm2(head2_t[...], mixed)
            sg = sigmoid(pre)
            hidden = pre * sg
            e2 = jnp.sum(proj2_col[...] * hidden, axis=0, keepdims=True)
            energy_row[...] = live * (e1 + e2)
            dpre = proj2_col[...] * live * (sg + hidden * (1.0 - sg))
            dmixed = mm2(head2_in[...], dpre)
            da2[...] = mm2(blend2_in[...], dmixed)

            du[...] = jnp.zeros((24, EDGES), F32)

            def backward2(cc, c):
                at = pl.multiple_of(cc * 32, 32)
                rows = [pl.ds(d * C + at, 32) for d in range(4)]
                da = da2[rows[0], :]
                for b in range(K):
                    here = slice(b * A, (b + 1) * A)
                    w0 = r2[rows[0], here]
                    through = da * r2[rows[1], here]
                    dsv_hi[rows[0], here], dsv_lo[rows[0], here] = halves(da * w0)
                    along = None
                    for d in range(3):
                        u = unit[d:d + 1, here]
                        v = sv[rows[1 + d], here]
                        along = u * v if along is None else along + u * v
                        dsv_hi[rows[1 + d], here], dsv_lo[rows[1 + d], here] = halves(u * through)
                        du[8 * d:8 * d + 8, here] += octets(through * v)
                    dr2_hi[rows[0], here], dr2_lo[rows[0], here] = halves(da * sv[rows[0], here])
                    dr2_hi[rows[1], here], dr2_lo[rows[1], here] = halves(da * along)
                return c

            lax.fori_loop(0, C // 32, backward2, 0)

            hot = onehot[:, 0:OWN]
            dproj = dot_nt(dsv_hi[...], hot) + dot_nt(dsv_lo[...], hot)
            dkept = [mm2(source2_s[...], dproj[d * C:(d + 1) * C]) for d in range(4)]
            dscalars = dkept[0] + jnp.concatenate(
                [dmixed + head1_col[...] * live, jnp.zeros((C, A), F32)], axis=1)
            dx = mm2(blend1_in[...], dscalars)
            dm = [dx[0:C]]
            for d in range(3):
                dm.append(mm2(change1_in[...], dkept[1 + d]) + 2.0 * vectors[d] * dx[C:2 * C])
            for d in range(4):
                row = slice(d * C, (d + 1) * C)
                dnodes[row, 0:A] = dm[d][:, 0:A]
                dnodes[row, A:2 * A] = lower_twice(dm[d][:, A:])
                dnodes[row, 2 * A:3 * A] = upper_twice(dm[d][:, A:])

            def backward1(cc, c):
                at = pl.multiple_of(cc * 32, 32)
                rows = [pl.ds(d * C + at, 32) for d in range(4)]
                for s, (first, last) in enumerate(SEGMENTS):
                    g = [dnodes[rows[d], s * A:(s + 1) * A] for d in range(4)]
                    for b in range(first, last):
                        here = slice(b * A, (b + 1) * A)
                        sender = lift[rows[0], here]
                        through = r1[rows[1], here] * sender
                        along = None
                        for d in range(3):
                            u = unit[d:d + 1, here]
                            along = u * g[1 + d] if along is None else along + u * g[1 + d]
                            du[8 * d:8 * d + 8, here] += octets(through * g[1 + d])
                        dr1_hi[rows[0], here], dr1_lo[rows[0], here] = halves(g[0] * sender)
                        dr1_hi[rows[1], here], dr1_lo[rows[1], here] = halves(along * sender)
                return c

            lax.fori_loop(0, C // 32, backward1, 0)

            def finish(two):
                def body(i, c):
                    here = chunk_of(i)
                    dpre1 = (dot(out1_in[...], dr1_hi[:, here]) + dot(out1_in[...], dr1_lo[:, here])) * sd1[:, here]
                    if two:
                        dpre2 = (dot(out2_in[...], dr2_hi[:, here]) + dot(out2_in[...], dr2_lo[:, here])) * sd2[:, here]
                        db = mm2(basis_b[...], jnp.concatenate([dpre1, dpre2], axis=0))
                    else:
                        db = mm2(basis1_in[...], dpre1)
                    on_distance = jnp.sum(db * slope[:, here], axis=0, keepdims=True)
                    on_unit = jnp.zeros((8, CHUNK), F32)
                    for d in range(3):
                        part = jnp.sum(du[8 * d:8 * d + 8, here], axis=0, keepdims=True)
                        on_unit = jnp.where(wide8 == d, part, on_unit)
                    u = unit[:, here]
                    rd = inverse[:, here]
                    on_distance = on_distance - jnp.sum(u * on_unit, axis=0, keepdims=True) * rd
                    dacross[:, here] = on_unit * rd + u * on_distance
                    return c
                return body

            lax.fori_loop(0, OWN // CHUNK, finish(True), 0)
            lax.fori_loop(OWN // CHUNK, EDGES // CHUNK, finish(False), 0)

            sums, spreads = [], []
            for first, last in SEGMENTS:
                total = dacross[:, first * A:(first + 1) * A]
                for b in range(first + 1, last):
                    total = total + dacross[:, b * A:(b + 1) * A]
                sums.append(total)
                here = slice(first * A, last * A)
                spreads.append(joined(dot_nt(thirds(dacross[:, here]), onehot[:, here])))
            xo, xl, xu = spreads
            lo = sums[1] + pltpu.roll(sums[1], 64, 1)
            up = sums[2] + pltpu.roll(sums[2], 64, 1)
            ghosts = xo[:, A:] - jnp.where(below, lo, up)
            b_out[it, 0, :, A:] = xl[:, A:]
            b_out[it, 0, :, :A] = jnp.zeros((8, A), F32)
            b_out[it, 1, :, :A] = xl[:, :A]
            b_out[it, 1, :, A:] = ghosts
            b_out[it, 2, :, :A] = xu[:, :A]
            b_out[it, 2, :, A:] = ghosts
            b_out[it, 3, :, A:] = xu[:, A:]
            b_out[it, 3, :, :A] = jnp.zeros((8, A), F32)
            for copy in b_copies(it):
                copy.start()
            for copy in b_copies(it):
                copy.wait()
            l2, l1, u1, u2 = [b_in[it, j] for j in range(4)]
            lists = jnp.where(below, u1[:, A:] + u2[:, A:] + xu[:, A:], l1[:, A:] + l2[:, A:] + xl[:, A:])
            gradient = xo[:, :A] - sums[0] + l1[:, :A] + u1[:, :A] + joined(dot_nt(thirds(lists), listhot[...]))
            frc[...] = -gradient
            half[...] = half[...] - 0.5 * TIMESTEP * gradient * inertia

            @pl.when(it < EVALS - 1)
            def _():
                advance(it + 1)
                for copy in a_copies(it + 1):
                    copy.start()

            return carry

        lax.fori_loop(0, EVALS, evaluate, 0)

        energy = jnp.broadcast_to(jnp.sum(energy_row[...], axis=1, keepdims=True), (8, A))
        c_out[0] = pos[...]
        c_out[1] = half[...]
        c_out[2] = jnp.where(rows8 == 3, energy, frc[...])
        for copy in c_copies():
            copy.start()
        lane = lax.broadcasted_iota(I32, (1, replicas), 1)
        level = levels_in[...]
        here = jnp.sum(jnp.where(lane == rep, level, 0.0), axis=1, keepdims=True)
        there = jnp.sum(
            jnp.where(lane == jnp.broadcast_to(target_in[...], (1, replicas)), level, 0.0), axis=1, keepdims=True)
        factor = jnp.broadcast_to(jnp.sqrt(here / there), (8, A))
        partner = jnp.broadcast_to(target_in[...], (8, A))
        for copy in c_copies():
            copy.wait()

        def chosen(d):
            return jnp.where(partner == rep - 1, c_in[0, d], jnp.where(partner == rep + 1, c_in[1, d], c_out[d]))

        pos_out[0] = chosen(0)[0:3]
        vel_out[0] = (chosen(1) * factor)[0:3]
        last = chosen(2)
        frc_out[0] = last[0:3]
        energy_out[...] = last[3:4, 0:1]

    return kernel


def solution(mesh):
    domains, replicas = mesh.shape["dom"], mesh.shape["rep"]

    def on_device(
        particle_locations, particle_speeds, acting_pulls, reciprocal_particle_inertia, particle_elements,
        domain_real_particles, halo_send_places, adjacency_places, filled_adjacency_places, exchange_target,
        thermal_levels, element_features, first_distance_expansion, first_distance_filter, first_source_projection,
        first_invariant_blend, first_directional_change, first_linear_potential_head, second_distance_expansion,
        second_distance_filter, second_source_projection, second_invariant_blend, final_head_intermediate,
        final_head_projection,
    ):
        f32 = lambda *shape: pltpu.VMEM(shape, F32)
        bf16 = lambda *shape: pltpu.VMEM(shape, BF16)
        dma = lambda *shape: pltpu.SemaphoreType.DMA(shape)
        scratch = [
            f32(8, A), f32(8, A), f32(8, A), f32(2 * K, A), bf16(2 * A, EDGES), bf16(A, A), f32(C, EDGES),
            f32(C, 2 * A), f32(C, C),
            bf16(C, 2 * C), bf16(C, C), bf16(C, C), bf16(C, C), bf16(C, C), bf16(16, C), bf16(128, 16), bf16(8, 128),
            bf16(2 * C, 128), bf16(2 * C, 128), f32(C, A), f32(16, A),
            f32(8, EDGES), f32(8, EDGES), f32(8, EDGES), f32(64, EDGES), f32(64, OWN), f32(2 * C, EDGES),
            f32(2 * C, OWN), f32(4 * C, OWN), f32(4 * C, 2 * A), f32(C, A), f32(C, A),
            bf16(4 * C, OWN), bf16(4 * C, OWN), bf16(2 * C, EDGES), bf16(2 * C, EDGES), bf16(2 * C, OWN),
            bf16(2 * C, OWN), f32(24, EDGES), f32(4 * C, 3 * A), f32(8, EDGES), f32(1, A),
            f32(2, 8, 2 * A), f32(2, 4, 8, 2 * A), f32(K, A), f32(2, K, A), f32(2, 4, 8, 2 * A), f32(2, 4, 8, 2 * A),
            f32(3, 8, A), f32(2, 3, 8, A),
            dma(2, 4), dma(2, 4), dma(2), dma(2), dma(2, 4), dma(2, 4), dma(2), dma(2),
        ]
        vmem = pl.BlockSpec(memory_space=pltpu.VMEM)
        return tuple(pl.pallas_call(
            make_kernel(domains, replicas),
            out_shape=[jax.ShapeDtypeStruct((1, 3, A), F32)] * 3 + [jax.ShapeDtypeStruct((1, 1), F32)],
            in_specs=[vmem] * 24,
            out_specs=[vmem] * 4,
            scratch_shapes=scratch,
            compiler_params=pltpu.CompilerParams(
                collective_id=0, has_side_effects=True, vmem_limit_bytes=56 * 1024 * 1024),
        )(
            particle_locations, particle_speeds, acting_pulls, reciprocal_particle_inertia.reshape(1, A),
            particle_elements.reshape(1, A), domain_real_particles, halo_send_places, adjacency_places,
            filled_adjacency_places, exchange_target.reshape(1, 1), thermal_levels.reshape(1, -1),
            element_features, first_distance_expansion, first_distance_filter, first_source_projection,
            first_invariant_blend, first_directional_change, first_linear_potential_head.reshape(1, C),
            second_distance_expansion, second_distance_filter, second_source_projection, second_invariant_blend,
            final_head_intermediate, final_head_projection.reshape(1, -1),
        ))

    split3, split2 = P("rep", None, "dom"), P("rep", "dom")
    return jax.shard_map(
        on_device, mesh=mesh,
        in_specs=(split3, split3, split3, P("dom"), P("dom"), split2, split3, split3, split2, P("rep")) + (P(),) * 14,
        out_specs=(split3, split3, split3, split2), check_vma=False)
```

```python
import math

import jax
import jax.numpy as jnp
from jax import lax
from jax.experimental import pallas as pl
from jax.experimental.pallas import tpu as pltpu
from jax.sharding import PartitionSpec as P

MESH = pl.DeviceIdType.MESH
F32 = jnp.float32
BF16 = jnp.bfloat16
I32 = jnp.int32

CUTOFF = 6.0
SOFTEN = 0.25
SLAB_WIDTH = 3.5
TIMESTEP = 0.4
EVALS = 2
C = 128
A = 128
K = 16
EDGES = 2 * K * A
OWN = K * A
CHUNK = 1024
OFFSETS = (-2, -1, 1, 2)
SEGMENTS = ((0, 16), (16, 24), (24, 32))

SIN_TERMS = [(-1) ** j * math.pi ** (2 * j + 1) / math.factorial(2 * j + 1) for j in range(7)]
COS_TERMS = [(-1) ** j * math.pi ** (2 * j) / math.factorial(2 * j) for j in range(7)]


def dot(a, b):
    return jnp.dot(a, b, preferred_element_type=F32)


def dot_nt(a, b):
    return lax.dot_general(a, b, (((1,), (1,)), ((), ())), preferred_element_type=F32)


def halves(x):
    hi = x.astype(BF16)
    return hi, (x - hi.astype(F32)).astype(BF16)


def mm2(w, x):
    hi, lo = halves(x)
    return dot(w, hi) + dot(w, lo)


def thirds(x):
    hi = x.astype(BF16).astype(F32)
    rest = x - hi
    mid = rest.astype(BF16).astype(F32)
    return jnp.concatenate([hi, mid, rest - mid], 0).astype(BF16)


def joined(g):
    return g[0:8] + g[8:16] + g[16:24]


def polynomial(terms, z):
    total = jnp.full_like(z, terms[-1])
    for term in terms[-2::-1]:
        total = total * z + term
    return total


def lanes_below_64(shape):
    return lax.broadcasted_iota(I32, shape, 1) < 64


def lower_twice(x):
    return jnp.where(lanes_below_64(x.shape), x, pltpu.roll(x, 64, 1))


def upper_twice(x):
    return jnp.where(lanes_below_64(x.shape), pltpu.roll(x, 64, 1), x)


def octets(x):
    return jnp.sum(x.reshape(x.shape[0] // 8, 8, x.shape[1]), axis=0)


def sigmoid(x):
    return 0.5 * jnp.tanh(0.5 * x) + 0.5


def make_kernel(domains, replicas):
    box = SLAB_WIDTH * domains

    def kernel(
        pos_in, vel_in, frc_in, inertia_in, species_in, count_in, halo_in, adj_in, filled_in, target_in, levels_in,
        table_in, basis1_in, out1_in, source1_in, blend1_in, change1_in, head1_in,
        basis2_in, out2_in, source2_in, blend2_in, head2_t, proj2_in,
        pos_out, vel_out, frc_out, energy_out,
        pos, half, frc, adj, onehot, listhot, lift, h0, tabf,
        blend1_t, change1_t, source2_t, source2_s, blend2_t, head2_n, basis_t, out1_t, out2_t,
        head1_col, proj2_col,
        unit, inverse, bessels, r1, r1d, r2, r2d, sv, nodes, acc2, da2,
        dsv, du, dnodes, dacross, energy_row,
        a_out, a_in, s_out, s_in, b_out, b_in, c_out, c_in,
        a_send, a_recv, s_send, s_recv, b_send, b_recv, c_send, c_recv,
    ):
        dom = lax.axis_index("dom")
        rep = lax.axis_index("rep")
        around = [lax.rem(dom + off + domains, domains) for off in OFFSETS]
        rep_up, rep_down = lax.rem(rep + 1, replicas), lax.rem(rep + replicas - 1, replicas)

        def a_copies(it):
            return [
                pltpu.make_async_remote_copy(
                    src_ref=a_out.at[it], dst_ref=a_in.at[it, 3 - j],
                    send_sem=a_send.at[it, j], recv_sem=a_recv.at[it, 3 - j],
                    device_id=(rep, around[j]), device_id_type=MESH)
                for j in range(4)
            ]

        def b_copies(it):
            return [
                pltpu.make_async_remote_copy(
                    src_ref=b_out.at[it, j], dst_ref=b_in.at[it, 3 - j],
                    send_sem=b_send.at[it, j], recv_sem=b_recv.at[it, 3 - j],
                    device_id=(rep, around[j]), device_id_type=MESH)
                for j in range(4)
            ]

        def s_copies():
            return [
                pltpu.make_async_remote_copy(
                    src_ref=s_out, dst_ref=s_in.at[1 - j],
                    send_sem=s_send.at[j], recv_sem=s_recv.at[1 - j],
                    device_id=(rep, around[1 + j]), device_id_type=MESH)
                for j in range(2)
            ]

        def c_copies():
            return [
                pltpu.make_async_remote_copy(
                    src_ref=c_out, dst_ref=c_in.at[j],
                    send_sem=c_send.at[j], recv_sem=c_recv.at[j],
                    device_id=(to, dom), device_id_type=MESH)
                for j, to in ((0, rep_up), (1, rep_down))
            ]

        barrier = pltpu.get_barrier_semaphore()
        for j in range(4):
            pl.semaphore_signal(barrier, inc=1, device_id=(rep, around[j]), device_id_type=MESH)
        for to in (rep_up, rep_down):
            pl.semaphore_signal(barrier, inc=1, device_id=(to, dom), device_id_type=MESH)

        rows8 = lax.broadcasted_iota(I32, (8, A), 0)
        inertia = jnp.broadcast_to(inertia_in[...], (8, A))
        live_row = lax.broadcasted_iota(I32, (1, A), 1) < jnp.broadcast_to(count_in[...], (1, A))
        live = live_row.astype(F32)

        for ref, source in ((pos, pos_in), (half, vel_in), (frc, frc_in)):
            ref[...] = jnp.zeros((8, A), F32)
            for d in range(3):
                ref[d:d + 1, :] = source[d]
        pos[3:4, :] = species_in[...].astype(F32)

        numbers = lax.broadcasted_iota(I32, (A, A), 0)
        listed = jnp.concatenate([halo_in[0, 1:2, :], halo_in[0, 0:1, :]], axis=1)
        listhot[...] = (numbers == jnp.broadcast_to(listed, (A, A))).astype(F32).astype(BF16)

        def advance(it):
            halfway = half[...] + 0.5 * TIMESTEP * frc[...] * inertia
            half[...] = halfway
            moved = pos[...] + TIMESTEP * halfway
            pos[...] = moved
            a_out[it, :, 0:A] = moved
            a_out[it, :, A:2 * A] = joined(dot(thirds(moved), listhot[...]))

        advance(0)
        used = (lax.broadcasted_iota(I32, (K, A), 0) < jnp.broadcast_to(filled_in[...], (K, A))) & jnp.broadcast_to(
            live_row, (K, A))
        coded = jnp.where(used, adj_in[0] + 1, 0).astype(F32)
        adj[0:K, :] = coded
        s_out[...] = dot(coded.astype(BF16), listhot[...])

        pl.semaphore_wait(barrier, 6)
        for copy in a_copies(0) + s_copies():
            copy.start()

        blend1_t[...] = blend1_in[...].astype(F32).T.astype(BF16)
        change1_t[...] = change1_in[...].astype(F32).T.astype(BF16)
        scaled2 = source2_in[...].astype(F32) * (1.0 / K)
        source2_s[...] = scaled2.astype(BF16)
        source2_t[...] = scaled2.T.astype(BF16)
        blend2_t[...] = blend2_in[...].astype(F32).T.astype(BF16)
        head2_n[...] = head2_t[...].astype(F32).T.astype(BF16)
        both = jnp.concatenate([basis1_in[...].astype(F32), basis2_in[...].astype(F32)], axis=1)
        twice = jnp.concatenate([both, both], axis=0)
        none = jnp.zeros_like(twice)
        basis_t[...] = jnp.concatenate(
            [jnp.concatenate([twice, none], axis=1), jnp.concatenate([none, twice], axis=1)], axis=0).T.astype(BF16)
        for ref, source in ((out1_t, out1_in), (out2_t, out2_in)):
            whole = source[...].astype(F32)
            ref[...] = jnp.concatenate([whole, whole], axis=0).T.astype(BF16)
        head1_col[...] = jnp.broadcast_to(head1_in[...].astype(F32), (A, C)).T
        proj2_col[...] = jnp.broadcast_to(proj2_in[...].astype(F32), (A, 16)).T
        tabf[...] = jnp.zeros((C, C), F32)
        tabf[0:table_in.shape[0], :] = table_in[...].astype(F32)
        table_t = tabf[...].T.astype(BF16)
        source1_t = (source1_in[...].astype(F32) * (1.0 / K)).T.astype(BF16)

        ordinals = (lax.broadcasted_iota(I32, (2 * A, A), 0) + 1).astype(F32)

        def fill(b, carry):
            row = jnp.broadcast_to(adj[pl.ds(b, 1), :], (2 * A, A))
            onehot[:, pl.ds(pl.multiple_of(b * A, A), A)] = (ordinals == row).astype(F32).astype(BF16)
            return carry

        lax.fori_loop(0, K, fill, 0)

        for copy in s_copies():
            copy.wait()
        lower, upper = s_in[0], s_in[1]
        below = lanes_below_64((8, A))
        adj[K:K + 8, :] = jnp.where(below, lower[0:8], pltpu.roll(lower[8:16], 64, 1))
        adj[K + 8:K + 16, :] = jnp.where(below, pltpu.roll(upper[0:8], 64, 1), upper[8:16])
        lax.fori_loop(K, 2 * K, fill, 0)

        def shifts(number):
            down = jnp.where(number == 0, -box, 0.0).astype(F32)
            up = jnp.where(number == domains - 1, box, 0.0).astype(F32)
            return jnp.where(rows8 == 0, jnp.where(below, down, up), 0.0)

        own_shift, lower_shift, upper_shift = shifts(dom), shifts(around[1]), shifts(around[2])

        def extended(it):
            l2, l1, u1, u2 = [a_in[it, j] for j in range(4)]
            own = a_out[it]
            e0 = jnp.concatenate([own[:, :A], jnp.where(below, l1[:, A:], u1[:, A:]) + own_shift], axis=1)
            el = jnp.concatenate([l1[:, :A], jnp.where(below, l2[:, A:], own[:, A:]) + lower_shift], axis=1)
            eu = jnp.concatenate([u1[:, :A], jnp.where(below, own[:, A:], u2[:, A:]) + upper_shift], axis=1)
            centres = (own[:, :A], lower_twice(l1[:, A:]), upper_twice(u1[:, A:]))
            return (e0, el, eu), centres

        def chunk_of(i):
            return pl.ds(pl.multiple_of(i * CHUNK, CHUNK), CHUNK)

        per = CHUNK // A
        chunk_ranges = [(a // per, b // per) for a, b in SEGMENTS]

        def evaluate(it, carry):
            for copy in a_copies(it):
                copy.wait()
            exts, centres = extended(it)

            @pl.when(it == 0)
            def _():
                for s, ext in enumerate(exts):
                    kinds = jnp.broadcast_to(ext[3:4, :], (C, 2 * A))
                    which = lax.broadcasted_iota(I32, (C, 2 * A), 0).astype(F32)
                    initial = dot(table_t, (kinds == which).astype(F32).astype(BF16))
                    if s == 0:
                        h0[...] = initial
                    lifted = dot(source1_t, initial.astype(BF16))
                    pair = jnp.concatenate(halves(lifted), axis=0)

                    def spread(i, c):
                        hot = onehot[:, chunk_of(i)]
                        both = dot(pair, hot)
                        lift[:, chunk_of(i)] = both[0:C] + both[C:2 * C]
                        return c

                    lax.fori_loop(*chunk_ranges[s], spread, 0)

            wide8 = lax.broadcasted_iota(I32, (8, OWN), 0)
            order = (wide8 + 1).astype(F32)
            spatial = wide8 < 3

            for s, (begin, end) in enumerate(((0, OWN), (OWN, EDGES))):
                if s == 0:
                    apart = [joined(dot(thirds(exts[0]), onehot[:, 0:OWN])) - jnp.concatenate([centres[0]] * K, axis=1)]
                else:
                    middle = (OWN + EDGES) // 2
                    apart = [
                        joined(dot(thirds(ext), onehot[:, a:b])) - jnp.concatenate([centre] * (K // 2), axis=1)
                        for ext, centre, a, b in (
                            (exts[1], centres[1], OWN, middle), (exts[2], centres[2], middle, EDGES))
                    ]
                across = jnp.where(spatial, jnp.concatenate(apart, axis=1), 0.0)
                squared = jnp.broadcast_to(jnp.sum(across * across, axis=0, keepdims=True), (8, OWN)) + SOFTEN
                rd = lax.rsqrt(squared)
                rd = rd * (1.5 - 0.5 * squared * rd * rd)
                t = jnp.minimum(squared * rd * (1.0 / CUTOFF), 1.0)
                y = order * t
                turns = jnp.floor(y + 0.5)
                r = y - turns
                sign = 1.0 - 2.0 * (turns - 2.0 * jnp.floor(0.5 * turns))
                z = r * r
                sine = sign * r * polynomial(SIN_TERMS, z)
                cosine = sign * polynomial(COS_TERMS, z)
                t2 = t * t
                t4 = t2 * t2
                envelope = 1.0 + t4 * t * (-21.0 + t * (35.0 - 15.0 * t))
                fall = -105.0 * t4 * (1.0 - t) * (1.0 - t)
                front = math.sqrt(2.0 / CUTOFF) * rd
                bessel = front * sine * envelope
                slope = front * (
                    order * (math.pi / CUTOFF) * cosine * envelope + sine * (fall * (1.0 / CUTOFF) - envelope * rd))
                unit[:, begin:end] = across * rd
                inverse[:, begin:end] = rd
                hi = bessel.astype(BF16).astype(F32)
                hi_slope = slope.astype(BF16).astype(F32)
                bessels[:, begin:end] = jnp.concatenate(
                    [hi, bessel - hi, hi_slope, slope - hi_slope], axis=0).astype(BF16)

            for i in range(EDGES // CHUNK):
                here = slice(i * CHUNK, (i + 1) * CHUNK)
                if here.start < OWN:
                    pre = dot(basis_t[...], bessels[:, here])
                    grow = pre[128:256]
                    pre = pre[0:128]
                else:
                    pre = dot(basis_t[0:64, :], bessels[:, here])
                    grow = dot(basis_t[128:192, :], bessels[:, here])
                sg = sigmoid(pre)
                hidden = pre * sg
                hi, lo = halves(hidden)
                dhi, dlo = halves((sg + hidden * (1.0 - sg)) * grow)
                r1[:, here] = dot(out1_t[...], jnp.concatenate([hi[0:64], lo[0:64]], axis=0))
                r1d[:, here] = dot(out1_t[...], jnp.concatenate([dhi[0:64], dlo[0:64]], axis=0))
                if here.start < OWN:
                    r2[:, here] = dot(out2_t[...], jnp.concatenate([hi[64:128], lo[64:128]], axis=0))
                    r2d[:, here] = dot(out2_t[...], jnp.concatenate([dhi[64:128], dlo[64:128]], axis=0))

            def messages(cc, c):
                at = pl.multiple_of(cc * 32, 32)
                sums = []
                for first, last in SEGMENTS:
                    m = [jnp.zeros((32, A), F32) for _ in range(4)]
                    for b in range(first, last):
                        here = slice(b * A, (b + 1) * A)
                        sender = lift[pl.ds(at, 32), here]
                        m[0] = m[0] + r1[pl.ds(at, 32), here] * sender
                        through = r1[pl.ds(C + at, 32), here] * sender
                        for d in range(3):
                            m[1 + d] = m[1 + d] + unit[d:d + 1, here] * through
                    sums.append(m)
                for d in range(4):
                    row = pl.ds(d * C + at, 32)
                    nodes[row, 0:A] = sums[0][d]
                    lo, up = sums[1][d], sums[2][d]
                    lo = lo + pltpu.roll(lo, 64, 1)
                    up = up + pltpu.roll(up, 64, 1)
                    nodes[row, A:2 * A] = jnp.where(lanes_below_64((32, A)), lo, up)
                return c

            lax.fori_loop(0, C // 32, messages, 0)

            vectors = [nodes[(1 + d) * C:(2 + d) * C, :] for d in range(3)]
            squares = vectors[0] * vectors[0] + vectors[1] * vectors[1] + vectors[2] * vectors[2]
            scalars = h0[...] + mm2(blend1_t[...], jnp.concatenate([nodes[0:C, :], squares], axis=0))
            e1 = jnp.sum(head1_col[...] * scalars[:, 0:A], axis=0, keepdims=True)
            kept = [scalars.astype(BF16)] + [mm2(change1_t[...], v).astype(BF16) for v in vectors]
            projected = jnp.concatenate([dot(source2_t[...], f) for f in kept], axis=0)
            sv_hi, sv_lo = halves(projected)

            def gather2(i, c):
                hot = onehot[:, chunk_of(i)]
                sv[:, chunk_of(i)] = dot(sv_hi, hot) + dot(sv_lo, hot)
                return c

            lax.fori_loop(0, OWN // CHUNK, gather2, 0)

            def messages2(cc, c):
                at = pl.multiple_of(cc * 32, 32)
                total = jnp.zeros((32, A), F32)
                for b in range(K):
                    here = slice(b * A, (b + 1) * A)
                    along = unit[0:1, here] * sv[pl.ds(C + at, 32), here]
                    along = along + unit[1:2, here] * sv[pl.ds(2 * C + at, 32), here]
                    along = along + unit[2:3, here] * sv[pl.ds(3 * C + at, 32), here]
                    total = total + r2[pl.ds(at, 32), here] * sv[pl.ds(at, 32), here]
                    total = total + r2[pl.ds(C + at, 32), here] * along
                acc2[pl.ds(at, 32), :] = total
                return c

            lax.fori_loop(0, C // 32, messages2, 0)

            mixed = kept[0][:, 0:A].astype(F32) + mm2(blend2_t[...], acc2[...])
            pre = mm2(head2_t[...], mixed)
            sg = sigmoid(pre)
            hidden = pre * sg
            e2 = jnp.sum(proj2_col[...] * hidden, axis=0, keepdims=True)
            energy_row[...] = live * (e1 + e2)
            dpre = proj2_col[...] * live * (sg + hidden * (1.0 - sg))
            dmixed = mm2(head2_n[...], dpre)
            da2[...] = mm2(blend2_in[...], dmixed)

            du[...] = jnp.zeros((32, EDGES), F32)

            def backward2(cc, c):
                at = pl.multiple_of(cc * 32, 32)
                rows = [pl.ds(d * C + at, 32) for d in range(4)]
                da = da2[rows[0], :]
                for b in range(K):
                    here = slice(b * A, (b + 1) * A)
                    w0 = r2[rows[0], here]
                    through = da * r2[rows[1], here]
                    dsv[rows[0], here] = (da * w0).astype(BF16)
                    along = None
                    for d in range(3):
                        u = unit[d:d + 1, here]
                        v = sv[rows[1 + d], here]
                        along = u * v if along is None else along + u * v
                        dsv[rows[1 + d], here] = (u * through).astype(BF16)
                        du[8 * d:8 * d + 8, here] += octets(through * v)
                    du[24:32, here] += octets(da * (r2d[rows[0], here] * sv[rows[0], here] + r2d[rows[1], here] * along))
                return c

            lax.fori_loop(0, C // 32, backward2, 0)

            dproj = dot_nt(dsv[...], onehot[:, 0:OWN])
            dkept = [mm2(source2_s[...], dproj[d * C:(d + 1) * C]) for d in range(4)]
            dscalars = dkept[0] + jnp.concatenate(
                [dmixed + head1_col[...] * live, jnp.zeros((C, A), F32)], axis=1)
            dx = mm2(blend1_in[...], dscalars)
            dm = [dx[0:C]]
            for d in range(3):
                dm.append(mm2(change1_in[...], dkept[1 + d]) + 2.0 * vectors[d] * dx[C:2 * C])
            for d in range(4):
                row = slice(d * C, (d + 1) * C)
                dnodes[row, 0:A] = dm[d][:, 0:A]
                dnodes[row, A:2 * A] = lower_twice(dm[d][:, A:])
                dnodes[row, 2 * A:3 * A] = upper_twice(dm[d][:, A:])

            def backward1(cc, c):
                at = pl.multiple_of(cc * 32, 32)
                rows = [pl.ds(d * C + at, 32) for d in range(4)]
                for s, (first, last) in enumerate(SEGMENTS):
                    g = [dnodes[rows[d], s * A:(s + 1) * A] for d in range(4)]
                    for b in range(first, last):
                        here = slice(b * A, (b + 1) * A)
                        sender = lift[rows[0], here]
                        through = r1[rows[1], here] * sender
                        along = None
                        for d in range(3):
                            u = unit[d:d + 1, here]
                            along = u * g[1 + d] if along is None else along + u * g[1 + d]
                            du[8 * d:8 * d + 8, here] += octets(through * g[1 + d])
                        du[24:32, here] += octets(sender * (g[0] * r1d[rows[0], here] + along * r1d[rows[1], here]))
                return c

            lax.fori_loop(0, C // 32, backward1, 0)

            for begin, end in ((0, OWN), (OWN, EDGES)):
                here = slice(begin, end)
                on_distance = jnp.sum(du[24:32, here], axis=0, keepdims=True)
                on_unit = jnp.zeros((8, OWN), F32)
                for d in range(3):
                    part = jnp.sum(du[8 * d:8 * d + 8, here], axis=0, keepdims=True)
                    on_unit = jnp.where(wide8 == d, part, on_unit)
                u = unit[:, here]
                rd = inverse[:, here]
                on_distance = on_distance - jnp.sum(u * on_unit, axis=0, keepdims=True) * rd
                dacross[:, here] = on_unit * rd + u * on_distance

            sums, spreads = [], []
            for first, last in SEGMENTS:
                total = dacross[:, first * A:(first + 1) * A]
                for b in range(first + 1, last):
                    total = total + dacross[:, b * A:(b + 1) * A]
                sums.append(total)
                here = slice(first * A, last * A)
                spreads.append(joined(dot_nt(thirds(dacross[:, here]), onehot[:, here])))
            xo, xl, xu = spreads
            lo = sums[1] + pltpu.roll(sums[1], 64, 1)
            up = sums[2] + pltpu.roll(sums[2], 64, 1)
            ghosts = xo[:, A:] - jnp.where(below, lo, up)
            b_out[it, 0, :, A:] = xl[:, A:]
            b_out[it, 0, :, :A] = jnp.zeros((8, A), F32)
            b_out[it, 1, :, :A] = xl[:, :A]
            b_out[it, 1, :, A:] = ghosts
            b_out[it, 2, :, :A] = xu[:, :A]
            b_out[it, 2, :, A:] = ghosts
            b_out[it, 3, :, A:] = xu[:, A:]
            b_out[it, 3, :, :A] = jnp.zeros((8, A), F32)
            for copy in b_copies(it):
                copy.start()
            for copy in b_copies(it):
                copy.wait()
            l2, l1, u1, u2 = [b_in[it, j] for j in range(4)]
            lists = jnp.where(below, u1[:, A:] + u2[:, A:] + xu[:, A:], l1[:, A:] + l2[:, A:] + xl[:, A:])
            gradient = xo[:, :A] - sums[0] + l1[:, :A] + u1[:, :A] + joined(dot_nt(thirds(lists), listhot[...]))
            frc[...] = -gradient
            half[...] = half[...] - 0.5 * TIMESTEP * gradient * inertia

            @pl.when(it < EVALS - 1)
            def _():
                advance(it + 1)
                for copy in a_copies(it + 1):
                    copy.start()

            return carry

        lax.fori_loop(0, EVALS, evaluate, 0)

        energy = jnp.broadcast_to(jnp.sum(energy_row[...], axis=1, keepdims=True), (8, A))
        c_out[0] = pos[...]
        c_out[1] = half[...]
        c_out[2] = jnp.where(rows8 == 3, energy, frc[...])
        for copy in c_copies():
            copy.start()
        lane = lax.broadcasted_iota(I32, (1, replicas), 1)
        level = levels_in[...]
        here = jnp.sum(jnp.where(lane == rep, level, 0.0), axis=1, keepdims=True)
        there = jnp.sum(
            jnp.where(lane == jnp.broadcast_to(target_in[...], (1, replicas)), level, 0.0), axis=1, keepdims=True)
        factor = jnp.broadcast_to(jnp.sqrt(here / there), (8, A))
        partner = jnp.broadcast_to(target_in[...], (8, A))
        for copy in c_copies():
            copy.wait()

        def chosen(d):
            return jnp.where(partner == rep - 1, c_in[0, d], jnp.where(partner == rep + 1, c_in[1, d], c_out[d]))

        first, second, last = chosen(0), chosen(1) * factor, chosen(2)
        for d in range(3):
            pos_out[d] = first[d:d + 1]
            vel_out[d] = second[d:d + 1]
            frc_out[d] = last[d:d + 1]
        energy_out[...] = last[3:4, 0:1]

    return kernel


def solution(mesh):
    domains, replicas = mesh.shape["dom"], mesh.shape["rep"]

    def on_device(
        particle_locations, particle_speeds, acting_pulls, reciprocal_particle_inertia, particle_elements,
        domain_real_particles, halo_send_places, adjacency_places, filled_adjacency_places, exchange_target,
        thermal_levels, element_features, first_distance_expansion, first_distance_filter, first_source_projection,
        first_invariant_blend, first_directional_change, first_linear_potential_head, second_distance_expansion,
        second_distance_filter, second_source_projection, second_invariant_blend, final_head_intermediate,
        final_head_projection,
    ):
        f32 = lambda *shape: pltpu.VMEM(shape, F32)
        bf16 = lambda *shape: pltpu.VMEM(shape, BF16)
        dma = lambda *shape: pltpu.SemaphoreType.DMA(shape)
        scratch = [
            f32(8, A), f32(8, A), f32(8, A), f32(2 * K, A), bf16(2 * A, EDGES), bf16(A, A), f32(C, EDGES),
            f32(C, 2 * A), f32(C, C),
            bf16(C, 2 * C), bf16(C, C), bf16(C, C), bf16(C, C), bf16(C, C), bf16(C, 16), bf16(256, 32),
            bf16(2 * C, 128), bf16(2 * C, 128), f32(C, A), f32(16, A),
            f32(8, EDGES), f32(8, EDGES), bf16(32, EDGES), f32(2 * C, EDGES), f32(2 * C, EDGES),
            f32(2 * C, OWN), f32(2 * C, OWN), f32(4 * C, OWN), f32(4 * C, 2 * A), f32(C, A), f32(C, A),
            bf16(4 * C, OWN), f32(32, EDGES), f32(4 * C, 3 * A), f32(8, EDGES), f32(1, A),
            f32(2, 8, 2 * A), f32(2, 4, 8, 2 * A), f32(K, A), f32(2, K, A), f32(2, 4, 8, 2 * A), f32(2, 4, 8, 2 * A),
            f32(3, 8, A), f32(2, 3, 8, A),
            dma(2, 4), dma(2, 4), dma(2), dma(2), dma(2, 4), dma(2, 4), dma(2), dma(2),
        ]
        vmem = pl.BlockSpec(memory_space=pltpu.VMEM)
        rowwise = lambda x: jnp.transpose(x, (1, 0, 2))
        outs = pl.pallas_call(
            make_kernel(domains, replicas),
            out_shape=[jax.ShapeDtypeStruct((3, 1, A), F32)] * 3 + [jax.ShapeDtypeStruct((1, 1), F32)],
            in_specs=[vmem] * 24,
            out_specs=[vmem] * 4,
            scratch_shapes=scratch,
            compiler_params=pltpu.CompilerParams(
                collective_id=0, has_side_effects=True, vmem_limit_bytes=56 * 1024 * 1024),
        )(
            rowwise(particle_locations), rowwise(particle_speeds), rowwise(acting_pulls),
            reciprocal_particle_inertia.reshape(1, A),
            particle_elements.reshape(1, A), domain_real_particles, halo_send_places, adjacency_places,
            filled_adjacency_places, exchange_target.reshape(1, 1), thermal_levels.reshape(1, -1),
            element_features, first_distance_expansion, first_distance_filter, first_source_projection,
            first_invariant_blend, first_directional_change, first_linear_potential_head.reshape(1, C),
            second_distance_expansion, second_distance_filter, second_source_projection, second_invariant_blend,
            final_head_intermediate.T, final_head_projection.reshape(1, -1),
        )
        return tuple(rowwise(x) for x in outs[:3]) + (outs[3],)

    split3, split2 = P("rep", None, "dom"), P("rep", "dom")
    return jax.shard_map(
        on_device, mesh=mesh,
        in_specs=(split3, split3, split3, P("dom"), P("dom"), split2, split3, split3, split2, P("rep")) + (P(),) * 14,
        out_specs=(split3, split3, split3, split2), check_vma=False)
```

```python
import math

import jax
import jax.numpy as jnp
from jax import lax
from jax.experimental import pallas as pl
from jax.experimental.pallas import tpu as pltpu
from jax.sharding import PartitionSpec as P

MESH = pl.DeviceIdType.MESH
F32 = jnp.float32
BF16 = jnp.bfloat16
I32 = jnp.int32

CUTOFF = 6.0
SOFTEN = 0.25
SLAB_WIDTH = 3.5
TIMESTEP = 0.4
EVALS = 2
C = 128
A = 128
K = 16
EDGES = 2 * K * A
OWN = K * A
CHUNK = 1024
OFFSETS = (-2, -1, 1, 2)
SEGMENTS = ((0, 16), (16, 24), (24, 32))

SIN_TERMS = [(-1) ** j * math.pi ** (2 * j + 1) / math.factorial(2 * j + 1) for j in range(7)]
COS_TERMS = [(-1) ** j * math.pi ** (2 * j) / math.factorial(2 * j) for j in range(7)]


def dot(a, b):
    return jnp.dot(a, b, preferred_element_type=F32)


def dot_nt(a, b):
    return lax.dot_general(a, b, (((1,), (1,)), ((), ())), preferred_element_type=F32)


def halves(x):
    hi = x.astype(BF16)
    return hi, (x - hi.astype(F32)).astype(BF16)


def mm2(w, x):
    hi, lo = halves(x)
    return dot(w, hi) + dot(w, lo)


def thirds(x):
    hi = x.astype(BF16).astype(F32)
    rest = x - hi
    mid = rest.astype(BF16).astype(F32)
    return jnp.concatenate([hi, mid, rest - mid], 0).astype(BF16)


def joined(g):
    return g[0:8] + g[8:16] + g[16:24]


def polynomial(terms, z):
    total = jnp.full_like(z, terms[-1])
    for term in terms[-2::-1]:
        total = total * z + term
    return total


def lanes_below_64(shape):
    return lax.broadcasted_iota(I32, shape, 1) < 64


def lower_twice(x):
    return jnp.where(lanes_below_64(x.shape), x, pltpu.roll(x, 64, 1))


def upper_twice(x):
    return jnp.where(lanes_below_64(x.shape), pltpu.roll(x, 64, 1), x)


def octets(x):
    return jnp.sum(x.reshape(x.shape[0] // 8, 8, x.shape[1]), axis=0)


def sigmoid(x):
    return 0.5 * jnp.tanh(0.5 * x) + 0.5


def make_kernel(domains, replicas):
    box = SLAB_WIDTH * domains

    def kernel(
        pos_in, vel_in, frc_in, inertia_in, species_in, count_in, halo_in, adj_in, filled_in, target_in, levels_in,
        table_in, basis1_in, out1_in, source1_in, blend1_in, change1_in, head1_in,
        basis2_in, out2_in, source2_in, blend2_in, head2_t, proj2_in,
        pos_out, vel_out, frc_out, energy_out,
        pos, half, frc, adj, onehot, listhot, lift, h0, tabf,
        blend1_t, change1_t, source2_t, source2_s, blend2_t, head2_n, basis_t, out1_t, out2_t,
        head1_col, proj2_col,
        unit, inverse, bessels, r1, r1d, r2, r2d, sv, nodes, acc2, da2,
        dsv, du, dnodes, dacross, energy_row,
        a_out, a_in, s_out, s_in, b_out, b_in, c_out, c_in,
        a_send, a_recv, s_send, s_recv, b_send, b_recv, c_send, c_recv,
    ):
        dom = lax.axis_index("dom")
        rep = lax.axis_index("rep")
        around = [lax.rem(dom + off + domains, domains) for off in OFFSETS]
        rep_up, rep_down = lax.rem(rep + 1, replicas), lax.rem(rep + replicas - 1, replicas)

        def a_copies(it):
            return [
                pltpu.make_async_remote_copy(
                    src_ref=a_out.at[it], dst_ref=a_in.at[it, 3 - j],
                    send_sem=a_send.at[it, j], recv_sem=a_recv.at[it, 3 - j],
                    device_id=(rep, around[j]), device_id_type=MESH)
                for j in range(4)
            ]

        def b_copies(it):
            return [
                pltpu.make_async_remote_copy(
                    src_ref=b_out.at[it, j], dst_ref=b_in.at[it, 3 - j],
                    send_sem=b_send.at[it, j], recv_sem=b_recv.at[it, 3 - j],
                    device_id=(rep, around[j]), device_id_type=MESH)
                for j in range(4)
            ]

        def s_copies():
            return [
                pltpu.make_async_remote_copy(
                    src_ref=s_out, dst_ref=s_in.at[1 - j],
                    send_sem=s_send.at[j], recv_sem=s_recv.at[1 - j],
                    device_id=(rep, around[1 + j]), device_id_type=MESH)
                for j in range(2)
            ]

        def c_copies():
            return [
                pltpu.make_async_remote_copy(
                    src_ref=c_out, dst_ref=c_in.at[j],
                    send_sem=c_send.at[j], recv_sem=c_recv.at[j],
                    device_id=(to, dom), device_id_type=MESH)
                for j, to in ((0, rep_up), (1, rep_down))
            ]

        barrier = pltpu.get_barrier_semaphore()
        for j in range(4):
            pl.semaphore_signal(barrier, inc=1, device_id=(rep, around[j]), device_id_type=MESH)
        for to in (rep_up, rep_down):
            pl.semaphore_signal(barrier, inc=1, device_id=(to, dom), device_id_type=MESH)

        rows8 = lax.broadcasted_iota(I32, (8, A), 0)
        inertia = jnp.broadcast_to(inertia_in[...], (8, A))
        live_row = lax.broadcasted_iota(I32, (1, A), 1) < jnp.broadcast_to(count_in[...], (1, A))
        live = live_row.astype(F32)

        for ref, source in ((pos, pos_in), (half, vel_in), (frc, frc_in)):
            ref[...] = jnp.zeros((8, A), F32)
            for d in range(3):
                ref[d:d + 1, :] = source[d]
        pos[3:4, :] = species_in[...].astype(F32)

        numbers = lax.broadcasted_iota(I32, (A, A), 0)
        listed = jnp.concatenate([halo_in[0, 1:2, :], halo_in[0, 0:1, :]], axis=1)
        listhot[...] = (numbers == jnp.broadcast_to(listed, (A, A))).astype(F32).astype(BF16)

        def advance(it):
            halfway = half[...] + 0.5 * TIMESTEP * frc[...] * inertia
            half[...] = halfway
            moved = pos[...] + TIMESTEP * halfway
            pos[...] = moved
            a_out[it, :, 0:A] = moved
            a_out[it, :, A:2 * A] = joined(dot(thirds(moved), listhot[...]))

        advance(0)
        used = (lax.broadcasted_iota(I32, (K, A), 0) < jnp.broadcast_to(filled_in[...], (K, A))) & jnp.broadcast_to(
            live_row, (K, A))
        coded = jnp.where(used, adj_in[0] + 1, 0).astype(F32)
        adj[0:K, :] = coded
        s_out[...] = dot(coded.astype(BF16), listhot[...])

        pl.semaphore_wait(barrier, 6)
        for copy in a_copies(0) + s_copies():
            copy.start()

        blend1_t[...] = blend1_in[...].astype(F32).T.astype(BF16)
        change1_t[...] = change1_in[...].astype(F32).T.astype(BF16)
        scaled2 = source2_in[...].astype(F32) * (1.0 / K)
        source2_s[...] = scaled2.astype(BF16)
        source2_t[...] = scaled2.T.astype(BF16)
        blend2_t[...] = blend2_in[...].astype(F32).T.astype(BF16)
        head2_n[...] = head2_t[...].astype(F32).T.astype(BF16)
        both = jnp.concatenate([basis1_in[...].astype(F32), basis2_in[...].astype(F32)], axis=1)
        twice = jnp.concatenate([both, both], axis=0)
        none = jnp.zeros_like(twice)
        basis_t[...] = jnp.concatenate(
            [jnp.concatenate([twice, none], axis=1), jnp.concatenate([none, twice], axis=1)], axis=0).T.astype(BF16)
        for ref, source in ((out1_t, out1_in), (out2_t, out2_in)):
            whole = source[...].astype(F32)
            ref[...] = jnp.concatenate([whole, whole], axis=0).T.astype(BF16)
        head1_col[...] = jnp.broadcast_to(head1_in[...].astype(F32), (A, C)).T
        proj2_col[...] = jnp.broadcast_to(proj2_in[...].astype(F32), (A, 16)).T
        tabf[...] = jnp.zeros((C, C), F32)
        tabf[0:table_in.shape[0], :] = table_in[...].astype(F32)
        table_t = tabf[...].T.astype(BF16)
        source1_t = (source1_in[...].astype(F32) * (1.0 / K)).T.astype(BF16)

        ordinals = (lax.broadcasted_iota(I32, (2 * A, A), 0) + 1).astype(F32)

        def fill(b, carry):
            row = jnp.broadcast_to(adj[pl.ds(b, 1), :], (2 * A, A))
            onehot[:, pl.ds(pl.multiple_of(b * A, A), A)] = (ordinals == row).astype(F32).astype(BF16)
            return carry

        lax.fori_loop(0, K, fill, 0)

        for copy in s_copies():
            copy.wait()
        lower, upper = s_in[0], s_in[1]
        below = lanes_below_64((8, A))
        adj[K:K + 8, :] = jnp.where(below, lower[0:8], pltpu.roll(lower[8:16], 64, 1))
        adj[K + 8:K + 16, :] = jnp.where(below, pltpu.roll(upper[0:8], 64, 1), upper[8:16])
        lax.fori_loop(K, 2 * K, fill, 0)

        def shifts(number):
            down = jnp.where(number == 0, -box, 0.0).astype(F32)
            up = jnp.where(number == domains - 1, box, 0.0).astype(F32)
            return jnp.where(rows8 == 0, jnp.where(below, down, up), 0.0)

        own_shift, lower_shift, upper_shift = shifts(dom), shifts(around[1]), shifts(around[2])

        def extended(it):
            l2, l1, u1, u2 = [a_in[it, j] for j in range(4)]
            own = a_out[it]
            e0 = jnp.concatenate([own[:, :A], jnp.where(below, l1[:, A:], u1[:, A:]) + own_shift], axis=1)
            el = jnp.concatenate([l1[:, :A], jnp.where(below, l2[:, A:], own[:, A:]) + lower_shift], axis=1)
            eu = jnp.concatenate([u1[:, :A], jnp.where(below, own[:, A:], u2[:, A:]) + upper_shift], axis=1)
            centres = (own[:, :A], lower_twice(l1[:, A:]), upper_twice(u1[:, A:]))
            return (e0, el, eu), centres

        def chunk_of(i):
            return pl.ds(pl.multiple_of(i * CHUNK, CHUNK), CHUNK)

        per = CHUNK // A
        chunk_ranges = [(a // per, b // per) for a, b in SEGMENTS]

        def evaluate(it, carry):
            for copy in a_copies(it):
                copy.wait()
            exts, centres = extended(it)

            @pl.when(it == 0)
            def _():
                for s, ext in enumerate(exts):
                    kinds = jnp.broadcast_to(ext[3:4, :], (C, 2 * A))
                    which = lax.broadcasted_iota(I32, (C, 2 * A), 0).astype(F32)
                    initial = dot(table_t, (kinds == which).astype(F32).astype(BF16))
                    if s == 0:
                        h0[...] = initial
                    lifted = dot(source1_t, initial.astype(BF16))
                    pair = jnp.concatenate(halves(lifted), axis=0)

                    def spread(i, c):
                        hot = onehot[:, chunk_of(i)]
                        both = dot(pair, hot)
                        lift[:, chunk_of(i)] = both[0:C] + both[C:2 * C]
                        return c

                    lax.fori_loop(*chunk_ranges[s], spread, 0, unroll=True)

            wide8 = lax.broadcasted_iota(I32, (8, OWN), 0)
            order = (wide8 + 1).astype(F32)
            spatial = wide8 < 3

            for s, (begin, end) in enumerate(((0, OWN), (OWN, EDGES))):
                if s == 0:
                    apart = [joined(dot(thirds(exts[0]), onehot[:, 0:OWN])) - jnp.concatenate([centres[0]] * K, axis=1)]
                else:
                    middle = (OWN + EDGES) // 2
                    apart = [
                        joined(dot(thirds(ext), onehot[:, a:b])) - jnp.concatenate([centre] * (K // 2), axis=1)
                        for ext, centre, a, b in (
                            (exts[1], centres[1], OWN, middle), (exts[2], centres[2], middle, EDGES))
                    ]
                across = jnp.where(spatial, jnp.concatenate(apart, axis=1), 0.0)
                squared = jnp.broadcast_to(jnp.sum(across * across, axis=0, keepdims=True), (8, OWN)) + SOFTEN
                rd = lax.rsqrt(squared)
                rd = rd * (1.5 - 0.5 * squared * rd * rd)
                t = jnp.minimum(squared * rd * (1.0 / CUTOFF), 1.0)
                y = order * t
                turns = jnp.floor(y + 0.5)
                r = y - turns
                sign = 1.0 - 2.0 * (turns - 2.0 * jnp.floor(0.5 * turns))
                z = r * r
                sine = sign * r * polynomial(SIN_TERMS, z)
                cosine = sign * polynomial(COS_TERMS, z)
                t2 = t * t
                t4 = t2 * t2
                envelope = 1.0 + t4 * t * (-21.0 + t * (35.0 - 15.0 * t))
                fall = -105.0 * t4 * (1.0 - t) * (1.0 - t)
                front = math.sqrt(2.0 / CUTOFF) * rd
                bessel = front * sine * envelope
                slope = front * (
                    order * (math.pi / CUTOFF) * cosine * envelope + sine * (fall * (1.0 / CUTOFF) - envelope * rd))
                unit[:, begin:end] = across * rd
                inverse[:, begin:end] = rd
                hi = bessel.astype(BF16).astype(F32)
                hi_slope = slope.astype(BF16).astype(F32)
                bessels[:, begin:end] = jnp.concatenate(
                    [hi, bessel - hi, hi_slope, slope - hi_slope], axis=0).astype(BF16)

            for i in range(EDGES // CHUNK):
                here = slice(i * CHUNK, (i + 1) * CHUNK)
                if here.start < OWN:
                    pre = dot(basis_t[...], bessels[:, here])
                    grow = pre[128:256]
                    pre = pre[0:128]
                else:
                    pre = dot(basis_t[0:64, :], bessels[:, here])
                    grow = dot(basis_t[128:192, :], bessels[:, here])
                sg = sigmoid(pre)
                hidden = pre * sg
                hi, lo = halves(hidden)
                dhi, dlo = halves((sg + hidden * (1.0 - sg)) * grow)
                r1[:, here] = dot(out1_t[...], jnp.concatenate([hi[0:64], lo[0:64]], axis=0))
                r1d[:, here] = dot(out1_t[...], jnp.concatenate([dhi[0:64], dlo[0:64]], axis=0))
                if here.start < OWN:
                    r2[:, here] = dot(out2_t[...], jnp.concatenate([hi[64:128], lo[64:128]], axis=0))
                    r2d[:, here] = dot(out2_t[...], jnp.concatenate([dhi[64:128], dlo[64:128]], axis=0))

            def messages(cc, c):
                at = pl.multiple_of(cc * 32, 32)
                sums = []
                for first, last in SEGMENTS:
                    m = [jnp.zeros((32, A), F32) for _ in range(4)]
                    for b in range(first, last):
                        here = slice(b * A, (b + 1) * A)
                        sender = lift[pl.ds(at, 32), here]
                        m[0] = m[0] + r1[pl.ds(at, 32), here] * sender
                        through = r1[pl.ds(C + at, 32), here] * sender
                        for d in range(3):
                            m[1 + d] = m[1 + d] + unit[d:d + 1, here] * through
                    sums.append(m)
                for d in range(4):
                    row = pl.ds(d * C + at, 32)
                    nodes[row, 0:A] = sums[0][d]
                    lo, up = sums[1][d], sums[2][d]
                    lo = lo + pltpu.roll(lo, 64, 1)
                    up = up + pltpu.roll(up, 64, 1)
                    nodes[row, A:2 * A] = jnp.where(lanes_below_64((32, A)), lo, up)
                return c

            lax.fori_loop(0, C // 32, messages, 0, unroll=True)

            vectors = [nodes[(1 + d) * C:(2 + d) * C, :] for d in range(3)]
            squares = vectors[0] * vectors[0] + vectors[1] * vectors[1] + vectors[2] * vectors[2]
            scalars = h0[...] + mm2(blend1_t[...], jnp.concatenate([nodes[0:C, :], squares], axis=0))
            e1 = jnp.sum(head1_col[...] * scalars[:, 0:A], axis=0, keepdims=True)
            kept = [scalars.astype(BF16)] + [mm2(change1_t[...], v).astype(BF16) for v in vectors]
            projected = jnp.concatenate([dot(source2_t[...], f) for f in kept], axis=0)
            sv_hi, sv_lo = halves(projected)

            def gather2(i, c):
                hot = onehot[:, chunk_of(i)]
                sv[:, chunk_of(i)] = dot(sv_hi, hot) + dot(sv_lo, hot)
                return c

            lax.fori_loop(0, OWN // CHUNK, gather2, 0, unroll=True)

            def messages2(cc, c):
                at = pl.multiple_of(cc * 32, 32)
                total = jnp.zeros((32, A), F32)
                for b in range(K):
                    here = slice(b * A, (b + 1) * A)
                    along = unit[0:1, here] * sv[pl.ds(C + at, 32), here]
                    along = along + unit[1:2, here] * sv[pl.ds(2 * C + at, 32), here]
                    along = along + unit[2:3, here] * sv[pl.ds(3 * C + at, 32), here]
                    total = total + r2[pl.ds(at, 32), here] * sv[pl.ds(at, 32), here]
                    total = total + r2[pl.ds(C + at, 32), here] * along
                acc2[pl.ds(at, 32), :] = total
                return c

            lax.fori_loop(0, C // 32, messages2, 0, unroll=True)

            mixed = kept[0][:, 0:A].astype(F32) + mm2(blend2_t[...], acc2[...])
            pre = mm2(head2_t[...], mixed)
            sg = sigmoid(pre)
            hidden = pre * sg
            e2 = jnp.sum(proj2_col[...] * hidden, axis=0, keepdims=True)
            energy_row[...] = live * (e1 + e2)
            dpre = proj2_col[...] * live * (sg + hidden * (1.0 - sg))
            dmixed = mm2(head2_n[...], dpre)
            da2[...] = mm2(blend2_in[...], dmixed)

            du[...] = jnp.zeros((32, EDGES), F32)

            def backward2(cc, c):
                at = pl.multiple_of(cc * 32, 32)
                rows = [pl.ds(d * C + at, 32) for d in range(4)]
                da = da2[rows[0], :]
                for b in range(K):
                    here = slice(b * A, (b + 1) * A)
                    w0 = r2[rows[0], here]
                    through = da * r2[rows[1], here]
                    dsv[rows[0], here] = (da * w0).astype(BF16)
                    along = None
                    for d in range(3):
                        u = unit[d:d + 1, here]
                        v = sv[rows[1 + d], here]
                        along = u * v if along is None else along + u * v
                        dsv[rows[1 + d], here] = (u * through).astype(BF16)
                        du[8 * d:8 * d + 8, here] += octets(through * v)
                    du[24:32, here] += octets(da * (r2d[rows[0], here] * sv[rows[0], here] + r2d[rows[1], here] * along))
                return c

            lax.fori_loop(0, C // 32, backward2, 0, unroll=True)

            dproj = jnp.concatenate(
                [dot_nt(dsv[2 * C * q:2 * C * (q + 1)], onehot[:, 0:OWN]) for q in range(2)], axis=0)
            dkept = [mm2(source2_s[...], dproj[d * C:(d + 1) * C]) for d in range(4)]
            dscalars = dkept[0] + jnp.concatenate(
                [dmixed + head1_col[...] * live, jnp.zeros((C, A), F32)], axis=1)
            dx = mm2(blend1_in[...], dscalars)
            dm = [dx[0:C]]
            for d in range(3):
                dm.append(mm2(change1_in[...], dkept[1 + d]) + 2.0 * vectors[d] * dx[C:2 * C])
            for d in range(4):
                row = slice(d * C, (d + 1) * C)
                dnodes[row, 0:A] = dm[d][:, 0:A]
                dnodes[row, A:2 * A] = lower_twice(dm[d][:, A:])
                dnodes[row, 2 * A:3 * A] = upper_twice(dm[d][:, A:])

            def backward1(cc, c):
                at = pl.multiple_of(cc * 32, 32)
                rows = [pl.ds(d * C + at, 32) for d in range(4)]
                for s, (first, last) in enumerate(SEGMENTS):
                    g = [dnodes[rows[d], s * A:(s + 1) * A] for d in range(4)]
                    for b in range(first, last):
                        here = slice(b * A, (b + 1) * A)
                        sender = lift[rows[0], here]
                        through = r1[rows[1], here] * sender
                        along = None
                        for d in range(3):
                            u = unit[d:d + 1, here]
                            along = u * g[1 + d] if along is None else along + u * g[1 + d]
                            du[8 * d:8 * d + 8, here] += octets(through * g[1 + d])
                        du[24:32, here] += octets(sender * (g[0] * r1d[rows[0], here] + along * r1d[rows[1], here]))
                return c

            lax.fori_loop(0, C // 32, backward1, 0, unroll=True)

            for begin, end in ((0, OWN), (OWN, EDGES)):
                here = slice(begin, end)
                on_distance = jnp.sum(du[24:32, here], axis=0, keepdims=True)
                on_unit = jnp.zeros((8, OWN), F32)
                for d in range(3):
                    part = jnp.sum(du[8 * d:8 * d + 8, here], axis=0, keepdims=True)
                    on_unit = jnp.where(wide8 == d, part, on_unit)
                u = unit[:, here]
                rd = inverse[:, here]
                on_distance = on_distance - jnp.sum(u * on_unit, axis=0, keepdims=True) * rd
                dacross[:, here] = on_unit * rd + u * on_distance

            sums, spreads = [], []
            for first, last in SEGMENTS:
                total = dacross[:, first * A:(first + 1) * A]
                for b in range(first + 1, last):
                    total = total + dacross[:, b * A:(b + 1) * A]
                sums.append(total)
                here = slice(first * A, last * A)
                spreads.append(joined(dot_nt(thirds(dacross[:, here]), onehot[:, here])))
            xo, xl, xu = spreads
            lo = sums[1] + pltpu.roll(sums[1], 64, 1)
            up = sums[2] + pltpu.roll(sums[2], 64, 1)
            ghosts = xo[:, A:] - jnp.where(below, lo, up)
            b_out[it, 0, :, A:] = xl[:, A:]
            b_out[it, 0, :, :A] = jnp.zeros((8, A), F32)
            b_out[it, 1, :, :A] = xl[:, :A]
            b_out[it, 1, :, A:] = ghosts
            b_out[it, 2, :, :A] = xu[:, :A]
            b_out[it, 2, :, A:] = ghosts
            b_out[it, 3, :, A:] = xu[:, A:]
            b_out[it, 3, :, :A] = jnp.zeros((8, A), F32)
            for copy in b_copies(it):
                copy.start()
            for copy in b_copies(it):
                copy.wait()
            l2, l1, u1, u2 = [b_in[it, j] for j in range(4)]
            lists = jnp.where(below, u1[:, A:] + u2[:, A:] + xu[:, A:], l1[:, A:] + l2[:, A:] + xl[:, A:])
            gradient = xo[:, :A] - sums[0] + l1[:, :A] + u1[:, :A] + joined(dot_nt(thirds(lists), listhot[...]))
            frc[...] = -gradient
            half[...] = half[...] - 0.5 * TIMESTEP * gradient * inertia

            @pl.when(it < EVALS - 1)
            def _():
                advance(it + 1)
                for copy in a_copies(it + 1):
                    copy.start()

            return carry

        lax.fori_loop(0, EVALS, evaluate, 0)

        energy = jnp.broadcast_to(jnp.sum(energy_row[...], axis=1, keepdims=True), (8, A))
        c_out[0] = pos[...]
        c_out[1] = half[...]
        c_out[2] = jnp.where(rows8 == 3, energy, frc[...])
        for copy in c_copies():
            copy.start()
        lane = lax.broadcasted_iota(I32, (1, replicas), 1)
        level = levels_in[...]
        here = jnp.sum(jnp.where(lane == rep, level, 0.0), axis=1, keepdims=True)
        there = jnp.sum(
            jnp.where(lane == jnp.broadcast_to(target_in[...], (1, replicas)), level, 0.0), axis=1, keepdims=True)
        factor = jnp.broadcast_to(jnp.sqrt(here / there), (8, A))
        partner = jnp.broadcast_to(target_in[...], (8, A))
        for copy in c_copies():
            copy.wait()

        def chosen(d):
            return jnp.where(partner == rep - 1, c_in[0, d], jnp.where(partner == rep + 1, c_in[1, d], c_out[d]))

        first, second, last = chosen(0), chosen(1) * factor, chosen(2)
        for d in range(3):
            pos_out[d] = first[d:d + 1]
            vel_out[d] = second[d:d + 1]
            frc_out[d] = last[d:d + 1]
        energy_out[...] = last[3:4, 0:1]

    return kernel


def solution(mesh):
    domains, replicas = mesh.shape["dom"], mesh.shape["rep"]

    def on_device(
        particle_locations, particle_speeds, acting_pulls, reciprocal_particle_inertia, particle_elements,
        domain_real_particles, halo_send_places, adjacency_places, filled_adjacency_places, exchange_target,
        thermal_levels, element_features, first_distance_expansion, first_distance_filter, first_source_projection,
        first_invariant_blend, first_directional_change, first_linear_potential_head, second_distance_expansion,
        second_distance_filter, second_source_projection, second_invariant_blend, final_head_intermediate,
        final_head_projection,
    ):
        f32 = lambda *shape: pltpu.VMEM(shape, F32)
        bf16 = lambda *shape: pltpu.VMEM(shape, BF16)
        dma = lambda *shape: pltpu.SemaphoreType.DMA(shape)
        scratch = [
            f32(8, A), f32(8, A), f32(8, A), f32(2 * K, A), bf16(2 * A, EDGES), bf16(A, A), f32(C, EDGES),
            f32(C, 2 * A), f32(C, C),
            bf16(C, 2 * C), bf16(C, C), bf16(C, C), bf16(C, C), bf16(C, C), bf16(C, 16), bf16(256, 32),
            bf16(2 * C, 128), bf16(2 * C, 128), f32(C, A), f32(16, A),
            f32(8, EDGES), f32(8, EDGES), bf16(32, EDGES), f32(2 * C, EDGES), f32(2 * C, EDGES),
            f32(2 * C, OWN), f32(2 * C, OWN), f32(4 * C, OWN), f32(4 * C, 2 * A), f32(C, A), f32(C, A),
            bf16(4 * C, OWN), f32(32, EDGES), f32(4 * C, 3 * A), f32(8, EDGES), f32(1, A),
            f32(2, 8, 2 * A), f32(2, 4, 8, 2 * A), f32(K, A), f32(2, K, A), f32(2, 4, 8, 2 * A), f32(2, 4, 8, 2 * A),
            f32(3, 8, A), f32(2, 3, 8, A),
            dma(2, 4), dma(2, 4), dma(2), dma(2), dma(2, 4), dma(2, 4), dma(2), dma(2),
        ]
        vmem = pl.BlockSpec(memory_space=pltpu.VMEM)
        rowwise = lambda x: jnp.transpose(x, (1, 0, 2))
        outs = pl.pallas_call(
            make_kernel(domains, replicas),
            out_shape=[jax.ShapeDtypeStruct((3, 1, A), F32)] * 3 + [jax.ShapeDtypeStruct((1, 1), F32)],
            in_specs=[vmem] * 24,
            out_specs=[vmem] * 4,
            scratch_shapes=scratch,
            compiler_params=pltpu.CompilerParams(
                collective_id=0, has_side_effects=True, vmem_limit_bytes=56 * 1024 * 1024),
        )(
            rowwise(particle_locations), rowwise(particle_speeds), rowwise(acting_pulls),
            reciprocal_particle_inertia.reshape(1, A),
            particle_elements.reshape(1, A), domain_real_particles, halo_send_places, adjacency_places,
            filled_adjacency_places, exchange_target.reshape(1, 1), thermal_levels.reshape(1, -1),
            element_features, first_distance_expansion, first_distance_filter, first_source_projection,
            first_invariant_blend, first_directional_change, first_linear_potential_head.reshape(1, C),
            second_distance_expansion, second_distance_filter, second_source_projection, second_invariant_blend,
            final_head_intermediate.T, final_head_projection.reshape(1, -1),
        )
        return tuple(rowwise(x) for x in outs[:3]) + (outs[3],)

    split3, split2 = P("rep", None, "dom"), P("rep", "dom")
    return jax.shard_map(
        on_device, mesh=mesh,
        in_specs=(split3, split3, split3, P("dom"), P("dom"), split2, split3, split3, split2, P("rep")) + (P(),) * 14,
        out_specs=(split3, split3, split3, split2), check_vma=False)
```

```python
import math

import jax
import jax.numpy as jnp
from jax import lax
from jax.experimental import pallas as pl
from jax.experimental.pallas import tpu as pltpu
from jax.sharding import PartitionSpec as P

MESH = pl.DeviceIdType.MESH
F32 = jnp.float32
BF16 = jnp.bfloat16
I32 = jnp.int32

CUTOFF = 6.0
SOFTEN = 0.25
SLAB_WIDTH = 3.5
TIMESTEP = 0.4
EVALS = 2
C = 128
A = 128
K = 16
EDGES = 2 * K * A
OWN = K * A
CHUNK = 1024
OFFSETS = (-2, -1, 1, 2)
SEGMENTS = ((0, 16), (16, 24), (24, 32))

SIN_TERMS = [(-1) ** j * math.pi ** (2 * j + 1) / math.factorial(2 * j + 1) for j in range(7)]
COS_TERMS = [(-1) ** j * math.pi ** (2 * j) / math.factorial(2 * j) for j in range(7)]


def dot(a, b):
    return jnp.dot(a, b, preferred_element_type=F32)


def dot_nt(a, b):
    return lax.dot_general(a, b, (((1,), (1,)), ((), ())), preferred_element_type=F32)


def halves(x):
    hi = x.astype(BF16)
    return hi, (x - hi.astype(F32)).astype(BF16)


def mm2(w, x):
    hi, lo = halves(x)
    return dot(w, hi) + dot(w, lo)


def thirds(x):
    hi = x.astype(BF16).astype(F32)
    rest = x - hi
    mid = rest.astype(BF16).astype(F32)
    return jnp.concatenate([hi, mid, rest - mid], 0).astype(BF16)


def joined(g):
    return g[0:8] + g[8:16] + g[16:24]


def polynomial(terms, z):
    total = jnp.full_like(z, terms[-1])
    for term in terms[-2::-1]:
        total = total * z + term
    return total


def lanes_below_64(shape):
    return lax.broadcasted_iota(I32, shape, 1) < 64


def lower_twice(x):
    return jnp.where(lanes_below_64(x.shape), x, pltpu.roll(x, 64, 1))


def upper_twice(x):
    return jnp.where(lanes_below_64(x.shape), pltpu.roll(x, 64, 1), x)


def octets(x):
    return jnp.sum(x.reshape(x.shape[0] // 8, 8, x.shape[1]), axis=0)


def sigmoid(x):
    return 0.5 * jnp.tanh(0.5 * x) + 0.5


def make_kernel(domains, replicas):
    box = SLAB_WIDTH * domains

    def kernel(
        pos_in, vel_in, frc_in, inertia_in, species_in, count_in, halo_in, adj_in, filled_in, target_in, levels_in,
        table_in, basis1_in, out1_in, source1_in, blend1_in, change1_in, head1_in,
        basis2_in, out2_in, source2_in, blend2_in, head2_t, proj2_in,
        pos_out, vel_out, frc_out, energy_out,
        pos, half, frc, adj, onehot, listhot, lift, h0, tabf,
        blend1_t, change1_t, source2_t, source2_s, blend2_t, head2_n, basis_t, out1_t, out2_t,
        head1_col, proj2_col,
        unit, inverse, bessels, r1, r1d, r2, r2d, sv, nodes, acc2, da2,
        dsv, du, dnodes, dacross, energy_row,
        a_out, a_in, s_out, s_in, b_out, b_in, c_in, l_out, l_in, o_out, o_in,
        a_send, a_recv, s_send, s_recv, b_send, b_recv, c_send, c_recv, l_send, l_recv, o_send, o_recv,
    ):
        dom = lax.axis_index("dom")
        rep = lax.axis_index("rep")
        around = [lax.rem(dom + off + domains, domains) for off in OFFSETS]
        rep_up, rep_down = lax.rem(rep + 1, replicas), lax.rem(rep + replicas - 1, replicas)

        def a_copies(it):
            return [
                pltpu.make_async_remote_copy(
                    src_ref=a_out.at[it], dst_ref=a_in.at[it, 3 - j],
                    send_sem=a_send.at[it, j], recv_sem=a_recv.at[it, 3 - j],
                    device_id=(rep, around[j]), device_id_type=MESH)
                for j in range(4)
            ]

        def b_copies(it):
            return [
                pltpu.make_async_remote_copy(
                    src_ref=b_out.at[it, j], dst_ref=b_in.at[it, 3 - j],
                    send_sem=b_send.at[it, j], recv_sem=b_recv.at[it, 3 - j],
                    device_id=(rep, around[j]), device_id_type=MESH)
                for j in range(4)
            ]

        def s_copies():
            return [
                pltpu.make_async_remote_copy(
                    src_ref=s_out, dst_ref=s_in.at[1 - j],
                    send_sem=s_send.at[j], recv_sem=s_recv.at[1 - j],
                    device_id=(rep, around[1 + j]), device_id_type=MESH)
                for j in range(2)
            ]

        sideways = ((0, rep_up), (1, rep_down))

        def l_copies():
            return [
                pltpu.make_async_remote_copy(
                    src_ref=l_out, dst_ref=l_in.at[k], send_sem=l_send.at[k], recv_sem=l_recv.at[k],
                    device_id=(to, dom), device_id_type=MESH)
                for k, to in sideways
            ]

        def c_copies():
            return [
                pltpu.make_async_remote_copy(
                    src_ref=b_out.at[EVALS - 1, j], dst_ref=c_in.at[k, 3 - j],
                    send_sem=c_send.at[k, j], recv_sem=c_recv.at[k, 3 - j],
                    device_id=(to, around[j]), device_id_type=MESH)
                for j in (1, 2, 0, 3) for k, to in sideways
            ] + [
                pltpu.make_async_remote_copy(
                    src_ref=o_out, dst_ref=o_in.at[k], send_sem=o_send.at[k], recv_sem=o_recv.at[k],
                    device_id=(to, dom), device_id_type=MESH)
                for k, to in sideways
            ]

        barrier = pltpu.get_barrier_semaphore()
        for j in range(4):
            pl.semaphore_signal(barrier, inc=1, device_id=(rep, around[j]), device_id_type=MESH)
        for to in (rep_up, rep_down):
            pl.semaphore_signal(barrier, inc=1, device_id=(to, dom), device_id_type=MESH)
            for j in range(4):
                pl.semaphore_signal(barrier, inc=1, device_id=(to, around[j]), device_id_type=MESH)

        rows8 = lax.broadcasted_iota(I32, (8, A), 0)
        inertia = jnp.broadcast_to(inertia_in[...], (8, A))
        live_row = lax.broadcasted_iota(I32, (1, A), 1) < jnp.broadcast_to(count_in[...], (1, A))
        live = live_row.astype(F32)

        for ref, source in ((pos, pos_in), (half, vel_in), (frc, frc_in)):
            ref[...] = jnp.zeros((8, A), F32)
            for d in range(3):
                ref[d:d + 1, :] = source[d]
        pos[3:4, :] = species_in[...].astype(F32)

        numbers = lax.broadcasted_iota(I32, (A, A), 0)
        listed = jnp.concatenate([halo_in[0, 1:2, :], halo_in[0, 0:1, :]], axis=1)
        l_out[...] = jnp.broadcast_to(listed, (8, A)).astype(F32)
        listhot[...] = (numbers == jnp.broadcast_to(listed, (A, A))).astype(F32).astype(BF16)

        def advance(it):
            halfway = half[...] + 0.5 * TIMESTEP * frc[...] * inertia
            half[...] = halfway
            moved = pos[...] + TIMESTEP * halfway
            pos[...] = moved
            a_out[it, :, 0:A] = moved
            a_out[it, :, A:2 * A] = joined(dot(thirds(moved), listhot[...]))

        advance(0)
        used = (lax.broadcasted_iota(I32, (K, A), 0) < jnp.broadcast_to(filled_in[...], (K, A))) & jnp.broadcast_to(
            live_row, (K, A))
        coded = jnp.where(used, adj_in[0] + 1, 0).astype(F32)
        adj[0:K, :] = coded
        s_out[...] = dot(coded.astype(BF16), listhot[...])

        pl.semaphore_wait(barrier, 14)
        for copy in a_copies(0) + s_copies() + l_copies():
            copy.start()

        blend1_t[...] = blend1_in[...].astype(F32).T.astype(BF16)
        change1_t[...] = change1_in[...].astype(F32).T.astype(BF16)
        scaled2 = source2_in[...].astype(F32) * (1.0 / K)
        source2_s[...] = scaled2.astype(BF16)
        source2_t[...] = scaled2.T.astype(BF16)
        blend2_t[...] = blend2_in[...].astype(F32).T.astype(BF16)
        head2_n[...] = head2_t[...].astype(F32).T.astype(BF16)
        both = jnp.concatenate([basis1_in[...].astype(F32), basis2_in[...].astype(F32)], axis=1)
        twice = jnp.concatenate([both, both], axis=0)
        none = jnp.zeros_like(twice)
        basis_t[...] = jnp.concatenate(
            [jnp.concatenate([twice, none], axis=1), jnp.concatenate([none, twice], axis=1)], axis=0).T.astype(BF16)
        for ref, source in ((out1_t, out1_in), (out2_t, out2_in)):
            whole = source[...].astype(F32)
            ref[...] = jnp.concatenate([whole, whole], axis=0).T.astype(BF16)
        head1_col[...] = jnp.broadcast_to(head1_in[...].astype(F32), (A, C)).T
        proj2_col[...] = jnp.broadcast_to(proj2_in[...].astype(F32), (A, 16)).T
        tabf[...] = jnp.zeros((C, C), F32)
        tabf[0:table_in.shape[0], :] = table_in[...].astype(F32)
        table_t = tabf[...].T.astype(BF16)
        source1_t = (source1_in[...].astype(F32) * (1.0 / K)).T.astype(BF16)

        ordinals = (lax.broadcasted_iota(I32, (2 * A, A), 0) + 1).astype(F32)

        def fill(b, carry):
            row = jnp.broadcast_to(adj[pl.ds(b, 1), :], (2 * A, A))
            onehot[:, pl.ds(pl.multiple_of(b * A, A), A)] = (ordinals == row).astype(F32).astype(BF16)
            return carry

        lax.fori_loop(0, K, fill, 0)

        for copy in s_copies():
            copy.wait()
        lower, upper = s_in[0], s_in[1]
        below = lanes_below_64((8, A))
        adj[K:K + 8, :] = jnp.where(below, lower[0:8], pltpu.roll(lower[8:16], 64, 1))
        adj[K + 8:K + 16, :] = jnp.where(below, pltpu.roll(upper[0:8], 64, 1), upper[8:16])
        lax.fori_loop(K, 2 * K, fill, 0)

        def shifts(number):
            down = jnp.where(number == 0, -box, 0.0).astype(F32)
            up = jnp.where(number == domains - 1, box, 0.0).astype(F32)
            return jnp.where(rows8 == 0, jnp.where(below, down, up), 0.0)

        own_shift, lower_shift, upper_shift = shifts(dom), shifts(around[1]), shifts(around[2])

        def extended(it):
            l2, l1, u1, u2 = [a_in[it, j] for j in range(4)]
            own = a_out[it]
            e0 = jnp.concatenate([own[:, :A], jnp.where(below, l1[:, A:], u1[:, A:]) + own_shift], axis=1)
            el = jnp.concatenate([l1[:, :A], jnp.where(below, l2[:, A:], own[:, A:]) + lower_shift], axis=1)
            eu = jnp.concatenate([u1[:, :A], jnp.where(below, own[:, A:], u2[:, A:]) + upper_shift], axis=1)
            centres = (own[:, :A], lower_twice(l1[:, A:]), upper_twice(u1[:, A:]))
            return (e0, el, eu), centres

        def chunk_of(i):
            return pl.ds(pl.multiple_of(i * CHUNK, CHUNK), CHUNK)

        per = CHUNK // A
        chunk_ranges = [(a // per, b // per) for a, b in SEGMENTS]

        def assembled(parts, own, hot):
            l2, l1, u1, u2 = parts
            lists = jnp.where(below, u1[:, A:] + u2[:, A:], l1[:, A:] + l2[:, A:]) + own[:, A:2 * A]
            return own[:, 0:A] + l1[:, :A] + u1[:, :A] + joined(dot_nt(thirds(lists), hot))

        def evaluate(it, carry):
            for copy in a_copies(it):
                copy.wait()
            exts, centres = extended(it)

            @pl.when(it == 0)
            def _():
                for s, ext in enumerate(exts):
                    kinds = jnp.broadcast_to(ext[3:4, :], (C, 2 * A))
                    which = lax.broadcasted_iota(I32, (C, 2 * A), 0).astype(F32)
                    initial = dot(table_t, (kinds == which).astype(F32).astype(BF16))
                    if s == 0:
                        h0[...] = initial
                    lifted = dot(source1_t, initial.astype(BF16))
                    pair = jnp.concatenate(halves(lifted), axis=0)

                    def spread(i, c):
                        hot = onehot[:, chunk_of(i)]
                        both = dot(pair, hot)
                        lift[:, chunk_of(i)] = both[0:C] + both[C:2 * C]
                        return c

                    lax.fori_loop(*chunk_ranges[s], spread, 0, unroll=True)

            wide8 = lax.broadcasted_iota(I32, (8, OWN), 0)
            order = (wide8 + 1).astype(F32)
            spatial = wide8 < 3

            for s, (begin, end) in enumerate(((0, OWN), (OWN, EDGES))):
                if s == 0:
                    apart = [joined(dot(thirds(exts[0]), onehot[:, 0:OWN])) - jnp.concatenate([centres[0]] * K, axis=1)]
                else:
                    middle = (OWN + EDGES) // 2
                    apart = [
                        joined(dot(thirds(ext), onehot[:, a:b])) - jnp.concatenate([centre] * (K // 2), axis=1)
                        for ext, centre, a, b in (
                            (exts[1], centres[1], OWN, middle), (exts[2], centres[2], middle, EDGES))
                    ]
                across = jnp.where(spatial, jnp.concatenate(apart, axis=1), 0.0)
                squared = jnp.broadcast_to(jnp.sum(across * across, axis=0, keepdims=True), (8, OWN)) + SOFTEN
                rd = lax.rsqrt(squared)
                rd = rd * (1.5 - 0.5 * squared * rd * rd)
                t = jnp.minimum(squared * rd * (1.0 / CUTOFF), 1.0)
                y = order * t
                turns = jnp.floor(y + 0.5)
                r = y - turns
                sign = 1.0 - 2.0 * (turns - 2.0 * jnp.floor(0.5 * turns))
                z = r * r
                sine = sign * r * polynomial(SIN_TERMS, z)
                cosine = sign * polynomial(COS_TERMS, z)
                t2 = t * t
                t4 = t2 * t2
                envelope = 1.0 + t4 * t * (-21.0 + t * (35.0 - 15.0 * t))
                fall = -105.0 * t4 * (1.0 - t) * (1.0 - t)
                front = math.sqrt(2.0 / CUTOFF) * rd
                bessel = front * sine * envelope
                slope = front * (
                    order * (math.pi / CUTOFF) * cosine * envelope + sine * (fall * (1.0 / CUTOFF) - envelope * rd))
                unit[:, begin:end] = across * rd
                inverse[:, begin:end] = rd
                hi = bessel.astype(BF16).astype(F32)
                hi_slope = slope.astype(BF16).astype(F32)
                bessels[:, begin:end] = jnp.concatenate(
                    [hi, bessel - hi, hi_slope, slope - hi_slope], axis=0).astype(BF16)

            for i in range(EDGES // CHUNK):
                here = slice(i * CHUNK, (i + 1) * CHUNK)
                if here.start < OWN:
                    pre = dot(basis_t[...], bessels[:, here])
                    grow = pre[128:256]
                    pre = pre[0:128]
                else:
                    pre = dot(basis_t[0:64, :], bessels[:, here])
                    grow = dot(basis_t[128:192, :], bessels[:, here])
                sg = sigmoid(pre)
                hidden = pre * sg
                hi, lo = halves(hidden)
                dhi, dlo = halves((sg + hidden * (1.0 - sg)) * grow)
                r1[:, here] = dot(out1_t[...], jnp.concatenate([hi[0:64], lo[0:64]], axis=0))
                r1d[:, here] = dot(out1_t[...], jnp.concatenate([dhi[0:64], dlo[0:64]], axis=0))
                if here.start < OWN:
                    r2[:, here] = dot(out2_t[...], jnp.concatenate([hi[64:128], lo[64:128]], axis=0))
                    r2d[:, here] = dot(out2_t[...], jnp.concatenate([dhi[64:128], dlo[64:128]], axis=0))

            def messages(cc, c):
                at = pl.multiple_of(cc * 32, 32)
                sums = []
                for first, last in SEGMENTS:
                    m = [jnp.zeros((32, A), F32) for _ in range(4)]
                    for b in range(first, last):
                        here = slice(b * A, (b + 1) * A)
                        sender = lift[pl.ds(at, 32), here]
                        m[0] = m[0] + r1[pl.ds(at, 32), here] * sender
                        through = r1[pl.ds(C + at, 32), here] * sender
                        for d in range(3):
                            m[1 + d] = m[1 + d] + unit[d:d + 1, here] * through
                    sums.append(m)
                for d in range(4):
                    row = pl.ds(d * C + at, 32)
                    nodes[row, 0:A] = sums[0][d]
                    lo, up = sums[1][d], sums[2][d]
                    lo = lo + pltpu.roll(lo, 64, 1)
                    up = up + pltpu.roll(up, 64, 1)
                    nodes[row, A:2 * A] = jnp.where(lanes_below_64((32, A)), lo, up)
                return c

            lax.fori_loop(0, C // 32, messages, 0, unroll=True)

            vectors = [nodes[(1 + d) * C:(2 + d) * C, :] for d in range(3)]
            squares = vectors[0] * vectors[0] + vectors[1] * vectors[1] + vectors[2] * vectors[2]
            scalars = h0[...] + mm2(blend1_t[...], jnp.concatenate([nodes[0:C, :], squares], axis=0))
            e1 = jnp.sum(head1_col[...] * scalars[:, 0:A], axis=0, keepdims=True)
            kept = [scalars.astype(BF16)] + [mm2(change1_t[...], v).astype(BF16) for v in vectors]
            projected = jnp.concatenate([dot(source2_t[...], f) for f in kept], axis=0)
            sv_hi, sv_lo = halves(projected)

            def gather2(i, c):
                hot = onehot[:, chunk_of(i)]
                sv[:, chunk_of(i)] = dot(sv_hi, hot) + dot(sv_lo, hot)
                return c

            lax.fori_loop(0, OWN // CHUNK, gather2, 0, unroll=True)

            def messages2(cc, c):
                at = pl.multiple_of(cc * 32, 32)
                total = jnp.zeros((32, A), F32)
                for b in range(K):
                    here = slice(b * A, (b + 1) * A)
                    along = unit[0:1, here] * sv[pl.ds(C + at, 32), here]
                    along = along + unit[1:2, here] * sv[pl.ds(2 * C + at, 32), here]
                    along = along + unit[2:3, here] * sv[pl.ds(3 * C + at, 32), here]
                    total = total + r2[pl.ds(at, 32), here] * sv[pl.ds(at, 32), here]
                    total = total + r2[pl.ds(C + at, 32), here] * along
                acc2[pl.ds(at, 32), :] = total
                return c

            lax.fori_loop(0, C // 32, messages2, 0, unroll=True)

            mixed = kept[0][:, 0:A].astype(F32) + mm2(blend2_t[...], acc2[...])
            pre = mm2(head2_t[...], mixed)
            sg = sigmoid(pre)
            hidden = pre * sg
            e2 = jnp.sum(proj2_col[...] * hidden, axis=0, keepdims=True)
            energy_row[...] = live * (e1 + e2)
            dpre = proj2_col[...] * live * (sg + hidden * (1.0 - sg))
            dmixed = mm2(head2_n[...], dpre)
            da2[...] = mm2(blend2_in[...], dmixed)

            du[...] = jnp.zeros((32, EDGES), F32)

            def backward2(cc, c):
                at = pl.multiple_of(cc * 32, 32)
                rows = [pl.ds(d * C + at, 32) for d in range(4)]
                da = da2[rows[0], :]
                for b in range(K):
                    here = slice(b * A, (b + 1) * A)
                    w0 = r2[rows[0], here]
                    through = da * r2[rows[1], here]
                    dsv[rows[0], here] = (da * w0).astype(BF16)
                    along = None
                    for d in range(3):
                        u = unit[d:d + 1, here]
                        v = sv[rows[1 + d], here]
                        along = u * v if along is None else along + u * v
                        dsv[rows[1 + d], here] = (u * through).astype(BF16)
                        du[8 * d:8 * d + 8, here] += octets(through * v)
                    du[24:32, here] += octets(da * (r2d[rows[0], here] * sv[rows[0], here] + r2d[rows[1], here] * along))
                return c

            lax.fori_loop(0, C // 32, backward2, 0, unroll=True)

            dproj = jnp.concatenate(
                [dot_nt(dsv[2 * C * q:2 * C * (q + 1)], onehot[:, 0:OWN]) for q in range(2)], axis=0)
            dkept = [mm2(source2_s[...], dproj[d * C:(d + 1) * C]) for d in range(4)]
            dscalars = dkept[0] + jnp.concatenate(
                [dmixed + head1_col[...] * live, jnp.zeros((C, A), F32)], axis=1)
            dx = mm2(blend1_in[...], dscalars)
            dm = [dx[0:C]]
            for d in range(3):
                dm.append(mm2(change1_in[...], dkept[1 + d]) + 2.0 * vectors[d] * dx[C:2 * C])
            for d in range(4):
                row = slice(d * C, (d + 1) * C)
                dnodes[row, 0:A] = dm[d][:, 0:A]
                dnodes[row, A:2 * A] = lower_twice(dm[d][:, A:])
                dnodes[row, 2 * A:3 * A] = upper_twice(dm[d][:, A:])

            def backward1(cc, c):
                at = pl.multiple_of(cc * 32, 32)
                rows = [pl.ds(d * C + at, 32) for d in range(4)]
                for s, (first, last) in enumerate(SEGMENTS):
                    g = [dnodes[rows[d], s * A:(s + 1) * A] for d in range(4)]
                    for b in range(first, last):
                        here = slice(b * A, (b + 1) * A)
                        sender = lift[rows[0], here]
                        through = r1[rows[1], here] * sender
                        along = None
                        for d in range(3):
                            u = unit[d:d + 1, here]
                            along = u * g[1 + d] if along is None else along + u * g[1 + d]
                            du[8 * d:8 * d + 8, here] += octets(through * g[1 + d])
                        du[24:32, here] += octets(sender * (g[0] * r1d[rows[0], here] + along * r1d[rows[1], here]))
                return c

            lax.fori_loop(0, C // 32, backward1, 0, unroll=True)

            for begin, end in ((0, OWN), (OWN, EDGES)):
                here = slice(begin, end)
                on_distance = jnp.sum(du[24:32, here], axis=0, keepdims=True)
                on_unit = jnp.zeros((8, OWN), F32)
                for d in range(3):
                    part = jnp.sum(du[8 * d:8 * d + 8, here], axis=0, keepdims=True)
                    on_unit = jnp.where(wide8 == d, part, on_unit)
                u = unit[:, here]
                rd = inverse[:, here]
                on_distance = on_distance - jnp.sum(u * on_unit, axis=0, keepdims=True) * rd
                dacross[:, here] = on_unit * rd + u * on_distance

            sums, spreads = [], []
            for first, last in SEGMENTS:
                total = dacross[:, first * A:(first + 1) * A]
                for b in range(first + 1, last):
                    total = total + dacross[:, b * A:(b + 1) * A]
                sums.append(total)
                here = slice(first * A, last * A)
                spreads.append(joined(dot_nt(thirds(dacross[:, here]), onehot[:, here])))
            xo, xl, xu = spreads
            lo = sums[1] + pltpu.roll(sums[1], 64, 1)
            up = sums[2] + pltpu.roll(sums[2], 64, 1)
            ghosts = xo[:, A:] - jnp.where(below, lo, up)
            b_out[it, 0, :, A:] = xl[:, A:]
            b_out[it, 0, :, :A] = jnp.zeros((8, A), F32)
            b_out[it, 1, :, :A] = xl[:, :A]
            b_out[it, 1, :, A:] = ghosts
            b_out[it, 2, :, :A] = xu[:, :A]
            b_out[it, 2, :, A:] = ghosts
            b_out[it, 3, :, A:] = xu[:, A:]
            b_out[it, 3, :, :A] = jnp.zeros((8, A), F32)
            o_out[:, 0:A] = xo[:, :A] - sums[0]
            o_out[:, A:2 * A] = jnp.where(below, xu[:, A:], xl[:, A:])
            for copy in b_copies(it):
                copy.start()

            @pl.when(it < EVALS - 1)
            def _():
                for copy in b_copies(it):
                    copy.wait()
                gradient = assembled([b_in[it, j] for j in range(4)], o_out[...], listhot[...])
                frc[...] = -gradient
                half[...] = half[...] - 0.5 * TIMESTEP * gradient * inertia
                advance(it + 1)
                for copy in a_copies(it + 1):
                    copy.start()

            return carry

        lax.fori_loop(0, EVALS, evaluate, 0)

        energy = jnp.broadcast_to(jnp.sum(energy_row[...], axis=1, keepdims=True), (8, A))
        o_out[:, 2 * A:3 * A] = jnp.where(rows8 == 3, energy, pos[...])
        o_out[:, 3 * A:4 * A] = half[...]
        for copy in c_copies():
            copy.start()
        lane = lax.broadcasted_iota(I32, (1, replicas), 1)
        level = levels_in[...]
        here = jnp.sum(jnp.where(lane == rep, level, 0.0), axis=1, keepdims=True)
        there = jnp.sum(
            jnp.where(lane == jnp.broadcast_to(target_in[...], (1, replicas)), level, 0.0), axis=1, keepdims=True)
        factor = jnp.broadcast_to(jnp.sqrt(here / there), (8, A))
        for copy in l_copies():
            copy.wait()

        def chosen(own, sent, shape):
            which = jnp.broadcast_to(target_in[...], shape)
            return jnp.where(which == rep - 1, sent[0], jnp.where(which == rep + 1, sent[1], own))

        columns = chosen(l_out[...], (l_in[0], l_in[1]), (8, A))
        hot = (numbers.astype(F32) == jnp.broadcast_to(columns[0:1], (A, A))).astype(F32).astype(BF16)
        for copy in b_copies(EVALS - 1) + c_copies():
            copy.wait()
        parts = [chosen(b_in[EVALS - 1, j], (c_in[0, j], c_in[1, j]), (8, 2 * A)) for j in range(4)]
        own = chosen(o_out[...], (o_in[0], o_in[1]), (8, 4 * A))
        gradient = assembled(parts, own, hot)
        first = own[:, 2 * A:3 * A]
        second = (own[:, 3 * A:4 * A] - 0.5 * TIMESTEP * gradient * inertia) * factor
        last = -gradient
        for d in range(3):
            pos_out[d] = first[d:d + 1]
            vel_out[d] = second[d:d + 1]
            frc_out[d] = last[d:d + 1]
        energy_out[...] = first[3:4, 0:1]

    return kernel


def solution(mesh):
    domains, replicas = mesh.shape["dom"], mesh.shape["rep"]

    def on_device(
        particle_locations, particle_speeds, acting_pulls, reciprocal_particle_inertia, particle_elements,
        domain_real_particles, halo_send_places, adjacency_places, filled_adjacency_places, exchange_target,
        thermal_levels, element_features, first_distance_expansion, first_distance_filter, first_source_projection,
        first_invariant_blend, first_directional_change, first_linear_potential_head, second_distance_expansion,
        second_distance_filter, second_source_projection, second_invariant_blend, final_head_intermediate,
        final_head_projection,
    ):
        f32 = lambda *shape: pltpu.VMEM(shape, F32)
        bf16 = lambda *shape: pltpu.VMEM(shape, BF16)
        dma = lambda *shape: pltpu.SemaphoreType.DMA(shape)
        scratch = [
            f32(8, A), f32(8, A), f32(8, A), f32(2 * K, A), bf16(2 * A, EDGES), bf16(A, A), f32(C, EDGES),
            f32(C, 2 * A), f32(C, C),
            bf16(C, 2 * C), bf16(C, C), bf16(C, C), bf16(C, C), bf16(C, C), bf16(C, 16), bf16(256, 32),
            bf16(2 * C, 128), bf16(2 * C, 128), f32(C, A), f32(16, A),
            f32(8, EDGES), f32(8, EDGES), bf16(32, EDGES), f32(2 * C, EDGES), f32(2 * C, EDGES),
            f32(2 * C, OWN), f32(2 * C, OWN), f32(4 * C, OWN), f32(4 * C, 2 * A), f32(C, A), f32(C, A),
            bf16(4 * C, OWN), f32(32, EDGES), f32(4 * C, 3 * A), f32(8, EDGES), f32(1, A),
            f32(2, 8, 2 * A), f32(2, 4, 8, 2 * A), f32(K, A), f32(2, K, A), f32(2, 4, 8, 2 * A), f32(2, 4, 8, 2 * A),
            f32(2, 4, 8, 2 * A), f32(8, A), f32(2, 8, A), f32(8, 4 * A), f32(2, 8, 4 * A),
            dma(2, 4), dma(2, 4), dma(2), dma(2), dma(2, 4), dma(2, 4), dma(2, 4), dma(2, 4),
            dma(2), dma(2), dma(2), dma(2),
        ]
        vmem = pl.BlockSpec(memory_space=pltpu.VMEM)
        rowwise = lambda x: jnp.transpose(x, (1, 0, 2))
        outs = pl.pallas_call(
            make_kernel(domains, replicas),
            out_shape=[jax.ShapeDtypeStruct((3, 1, A), F32)] * 3 + [jax.ShapeDtypeStruct((1, 1), F32)],
            in_specs=[vmem] * 24,
            out_specs=[vmem] * 4,
            scratch_shapes=scratch,
            compiler_params=pltpu.CompilerParams(
                collective_id=0, has_side_effects=True, vmem_limit_bytes=56 * 1024 * 1024),
        )(
            rowwise(particle_locations), rowwise(particle_speeds), rowwise(acting_pulls),
            reciprocal_particle_inertia.reshape(1, A),
            particle_elements.reshape(1, A), domain_real_particles, halo_send_places, adjacency_places,
            filled_adjacency_places, exchange_target.reshape(1, 1), thermal_levels.reshape(1, -1),
            element_features, first_distance_expansion, first_distance_filter, first_source_projection,
            first_invariant_blend, first_directional_change, first_linear_potential_head.reshape(1, C),
            second_distance_expansion, second_distance_filter, second_source_projection, second_invariant_blend,
            final_head_intermediate.T, final_head_projection.reshape(1, -1),
        )
        return tuple(rowwise(x) for x in outs[:3]) + (outs[3],)

    split3, split2 = P("rep", None, "dom"), P("rep", "dom")
    return jax.shard_map(
        on_device, mesh=mesh,
        in_specs=(split3, split3, split3, P("dom"), P("dom"), split2, split3, split3, split2, P("rep")) + (P(),) * 14,
        out_specs=(split3, split3, split3, split2), check_vma=False)
```

```python
import math

import jax
import jax.numpy as jnp
from jax import lax
from jax.experimental import pallas as pl
from jax.experimental.pallas import tpu as pltpu
from jax.sharding import PartitionSpec as P

MESH = pl.DeviceIdType.MESH
F32 = jnp.float32
BF16 = jnp.bfloat16
I32 = jnp.int32

CUTOFF = 6.0
SOFTEN = 0.25
SLAB_WIDTH = 3.5
TIMESTEP = 0.4
EVALS = 2
C = 128
A = 128
K = 16
EDGES = 2 * K * A
OWN = K * A
CHUNK = 1024
OFFSETS = (-2, -1, 1, 2)
SEGMENTS = ((0, 16), (16, 24), (24, 32))

SIN_TERMS = [(-1) ** j * math.pi ** (2 * j + 1) / math.factorial(2 * j + 1) for j in range(7)]
COS_TERMS = [(-1) ** j * math.pi ** (2 * j) / math.factorial(2 * j) for j in range(7)]


def dot(a, b):
    return jnp.dot(a, b, preferred_element_type=F32)


def dot_nt(a, b):
    return lax.dot_general(a, b, (((1,), (1,)), ((), ())), preferred_element_type=F32)


def halves(x):
    hi = x.astype(BF16)
    return hi, (x - hi.astype(F32)).astype(BF16)


def mm2(w, x):
    hi, lo = halves(x)
    return dot(w, hi) + dot(w, lo)


def thirds(x):
    hi = x.astype(BF16).astype(F32)
    rest = x - hi
    mid = rest.astype(BF16).astype(F32)
    return jnp.concatenate([hi, mid, rest - mid], 0).astype(BF16)


def joined(g):
    return g[0:8] + g[8:16] + g[16:24]


def polynomial(terms, z):
    total = jnp.full_like(z, terms[-1])
    for term in terms[-2::-1]:
        total = total * z + term
    return total


def lanes_below_64(shape):
    return lax.broadcasted_iota(I32, shape, 1) < 64


def lower_twice(x):
    return jnp.where(lanes_below_64(x.shape), x, pltpu.roll(x, 64, 1))


def upper_twice(x):
    return jnp.where(lanes_below_64(x.shape), pltpu.roll(x, 64, 1), x)


def octets(x):
    return jnp.sum(x.reshape(x.shape[0] // 8, 8, x.shape[1]), axis=0)


def sigmoid(x):
    return 0.5 * jnp.tanh(0.5 * x) + 0.5


def make_kernel(domains, replicas):
    box = SLAB_WIDTH * domains

    def kernel(
        pos_in, vel_in, frc_in, inertia_in, species_in, count_in, halo_in, adj_in, filled_in, target_in, levels_in,
        table_in, basis1_in, out1_in, source1_in, blend1_in, change1_in, head1_in,
        basis2_in, out2_in, source2_in, blend2_in, head2_t, proj2_in,
        pos_out, vel_out, frc_out, energy_out,
        pos, half, frc, adj, onehot, listhot, lift, h0, tabf,
        blend1_t, change1_t, source2_t, source2_s, blend2_t, head2_n, basis_t, out1_t, out2_t,
        head1_col, proj2_col,
        unit, inverse, bessels, r1, r1d, r2, r2d, sv, nodes, acc2, da2,
        dsv, du, dnodes, dacross, energy_row,
        a_out, a_in, s_out, s_in, b_out, b_in, c_in, l_out, l_in, o_out, o_in,
        a_send, a_recv, s_send, s_recv, b_send, b_recv, c_send, c_recv, l_send, l_recv, o_send, o_recv,
    ):
        dom = lax.axis_index("dom")
        rep = lax.axis_index("rep")
        around = [lax.rem(dom + off + domains, domains) for off in OFFSETS]
        rep_up, rep_down = lax.rem(rep + 1, replicas), lax.rem(rep + replicas - 1, replicas)

        def a_copies(it):
            return [
                pltpu.make_async_remote_copy(
                    src_ref=a_out.at[it], dst_ref=a_in.at[it, 3 - j],
                    send_sem=a_send.at[it, j], recv_sem=a_recv.at[it, 3 - j],
                    device_id=(rep, around[j]), device_id_type=MESH)
                for j in range(4)
            ]

        def b_copies(it):
            return [
                pltpu.make_async_remote_copy(
                    src_ref=b_out.at[it, j], dst_ref=b_in.at[it, 3 - j],
                    send_sem=b_send.at[it, j], recv_sem=b_recv.at[it, 3 - j],
                    device_id=(rep, around[j]), device_id_type=MESH)
                for j in range(4)
            ]

        def s_copies():
            return [
                pltpu.make_async_remote_copy(
                    src_ref=s_out, dst_ref=s_in.at[1 - j],
                    send_sem=s_send.at[j], recv_sem=s_recv.at[1 - j],
                    device_id=(rep, around[1 + j]), device_id_type=MESH)
                for j in range(2)
            ]

        sideways = ((0, rep_up), (1, rep_down))

        def l_copies():
            return [
                pltpu.make_async_remote_copy(
                    src_ref=l_out, dst_ref=l_in.at[k], send_sem=l_send.at[k], recv_sem=l_recv.at[k],
                    device_id=(to, dom), device_id_type=MESH)
                for k, to in sideways
            ]

        def c_copies():
            return [
                pltpu.make_async_remote_copy(
                    src_ref=b_out.at[EVALS - 1, j], dst_ref=c_in.at[k, 3 - j],
                    send_sem=c_send.at[k, j], recv_sem=c_recv.at[k, 3 - j],
                    device_id=(to, around[j]), device_id_type=MESH)
                for j in (1, 2, 0, 3) for k, to in sideways
            ] + [
                pltpu.make_async_remote_copy(
                    src_ref=o_out, dst_ref=o_in.at[k], send_sem=o_send.at[k], recv_sem=o_recv.at[k],
                    device_id=(to, dom), device_id_type=MESH)
                for k, to in sideways
            ]

        barrier = pltpu.get_barrier_semaphore()
        for j in range(4):
            pl.semaphore_signal(barrier, inc=1, device_id=(rep, around[j]), device_id_type=MESH)
        for to in (rep_up, rep_down):
            pl.semaphore_signal(barrier, inc=1, device_id=(to, dom), device_id_type=MESH)
            for j in range(4):
                pl.semaphore_signal(barrier, inc=1, device_id=(to, around[j]), device_id_type=MESH)

        rows8 = lax.broadcasted_iota(I32, (8, A), 0)
        inertia = jnp.broadcast_to(inertia_in[...], (8, A))
        live_row = lax.broadcasted_iota(I32, (1, A), 1) < jnp.broadcast_to(count_in[...], (1, A))
        live = live_row.astype(F32)

        for ref, source in ((pos, pos_in), (half, vel_in), (frc, frc_in)):
            ref[...] = jnp.zeros((8, A), F32)
            for d in range(3):
                ref[d:d + 1, :] = source[d]
        pos[3:4, :] = species_in[...].astype(F32)

        numbers = lax.broadcasted_iota(I32, (A, A), 0)
        listed = jnp.concatenate([halo_in[0, 1:2, :], halo_in[0, 0:1, :]], axis=1)
        l_out[...] = jnp.broadcast_to(listed, (8, A)).astype(F32)
        listhot[...] = (numbers == jnp.broadcast_to(listed, (A, A))).astype(F32).astype(BF16)

        def advance(it):
            halfway = half[...] + 0.5 * TIMESTEP * frc[...] * inertia
            half[...] = halfway
            moved = pos[...] + TIMESTEP * halfway
            pos[...] = moved
            a_out[it, :, 0:A] = moved
            a_out[it, :, A:2 * A] = joined(dot(thirds(moved), listhot[...]))

        advance(0)
        used = (lax.broadcasted_iota(I32, (K, A), 0) < jnp.broadcast_to(filled_in[...], (K, A))) & jnp.broadcast_to(
            live_row, (K, A))
        coded = jnp.where(used, adj_in[0] + 1, 0).astype(F32)
        adj[0:K, :] = coded
        s_out[...] = dot(coded.astype(BF16), listhot[...])

        pl.semaphore_wait(barrier, 14)
        for copy in a_copies(0) + s_copies() + l_copies():
            copy.start()

        blend1_t[...] = blend1_in[...].astype(F32).T.astype(BF16)
        change1_t[...] = change1_in[...].astype(F32).T.astype(BF16)
        scaled2 = source2_in[...].astype(F32) * (1.0 / K)
        source2_s[...] = scaled2.astype(BF16)
        source2_t[...] = scaled2.T.astype(BF16)
        blend2_t[...] = blend2_in[...].astype(F32).T.astype(BF16)
        head2_n[...] = head2_t[...].astype(F32).T.astype(BF16)
        both = jnp.concatenate([basis1_in[...].astype(F32), basis2_in[...].astype(F32)], axis=1)
        twice = jnp.concatenate([both, both], axis=0)
        none = jnp.zeros_like(twice)
        basis_t[...] = jnp.concatenate(
            [jnp.concatenate([twice, none], axis=1), jnp.concatenate([none, twice], axis=1)], axis=0).T.astype(BF16)
        for ref, source in ((out1_t, out1_in), (out2_t, out2_in)):
            whole = source[...].astype(F32)
            ref[...] = jnp.concatenate([whole, whole], axis=0).T.astype(BF16)
        head1_col[...] = jnp.broadcast_to(head1_in[...].astype(F32), (A, C)).T
        proj2_col[...] = jnp.broadcast_to(proj2_in[...].astype(F32), (A, 16)).T
        tabf[...] = jnp.zeros((C, C), F32)
        tabf[0:table_in.shape[0], :] = table_in[...].astype(F32)
        table_t = tabf[...].T.astype(BF16)
        source1_t = (source1_in[...].astype(F32) * (1.0 / K)).T.astype(BF16)

        ordinals = (lax.broadcasted_iota(I32, (2 * A, A), 0) + 1).astype(F32)

        def fill(b, carry):
            row = jnp.broadcast_to(adj[pl.ds(b, 1), :], (2 * A, A))
            onehot[:, pl.ds(pl.multiple_of(b * A, A), A)] = (ordinals == row).astype(F32).astype(BF16)
            return carry

        lax.fori_loop(0, K, fill, 0)

        for copy in s_copies():
            copy.wait()
        lower, upper = s_in[0], s_in[1]
        below = lanes_below_64((8, A))
        adj[K:K + 8, :] = jnp.where(below, lower[0:8], pltpu.roll(lower[8:16], 64, 1))
        adj[K + 8:K + 16, :] = jnp.where(below, pltpu.roll(upper[0:8], 64, 1), upper[8:16])
        lax.fori_loop(K, 2 * K, fill, 0)

        def shifts(number):
            down = jnp.where(number == 0, -box, 0.0).astype(F32)
            up = jnp.where(number == domains - 1, box, 0.0).astype(F32)
            return jnp.where(rows8 == 0, jnp.where(below, down, up), 0.0)

        own_shift, lower_shift, upper_shift = shifts(dom), shifts(around[1]), shifts(around[2])

        def extended(it):
            l2, l1, u1, u2 = [a_in[it, j] for j in range(4)]
            own = a_out[it]
            e0 = jnp.concatenate([own[:, :A], jnp.where(below, l1[:, A:], u1[:, A:]) + own_shift], axis=1)
            el = jnp.concatenate([l1[:, :A], jnp.where(below, l2[:, A:], own[:, A:]) + lower_shift], axis=1)
            eu = jnp.concatenate([u1[:, :A], jnp.where(below, own[:, A:], u2[:, A:]) + upper_shift], axis=1)
            centres = (own[:, :A], lower_twice(l1[:, A:]), upper_twice(u1[:, A:]))
            return (e0, el, eu), centres

        def chunk_of(i):
            return pl.ds(pl.multiple_of(i * CHUNK, CHUNK), CHUNK)

        per = CHUNK // A
        chunk_ranges = [(a // per, b // per) for a, b in SEGMENTS]

        def assembled(parts, own, hot):
            l2, l1, u1, u2 = parts
            lists = jnp.where(below, u1[:, A:] + u2[:, A:], l1[:, A:] + l2[:, A:]) + own[:, A:2 * A]
            return own[:, 0:A] + l1[:, :A] + u1[:, :A] + joined(dot_nt(thirds(lists), hot))

        def evaluate(it, carry):
            for copy in a_copies(it):
                copy.wait()
            exts, centres = extended(it)

            @pl.when(it == 0)
            def _():
                for s, ext in enumerate(exts):
                    kinds = jnp.broadcast_to(ext[3:4, :], (C, 2 * A))
                    which = lax.broadcasted_iota(I32, (C, 2 * A), 0).astype(F32)
                    initial = dot(table_t, (kinds == which).astype(F32).astype(BF16))
                    if s == 0:
                        h0[...] = initial
                    lifted = dot(source1_t, initial.astype(BF16))
                    pair = jnp.concatenate(halves(lifted), axis=0)

                    def spread(i, c):
                        hot = onehot[:, chunk_of(i)]
                        both = dot(pair, hot)
                        lift[:, chunk_of(i)] = both[0:C] + both[C:2 * C]
                        return c

                    lax.fori_loop(*chunk_ranges[s], spread, 0, unroll=True)

            wide8 = lax.broadcasted_iota(I32, (8, OWN), 0)
            order = (wide8 + 1).astype(F32)
            spatial = wide8 < 3

            for s, (begin, end) in enumerate(((0, OWN), (OWN, EDGES))):
                if s == 0:
                    apart = [joined(dot(thirds(exts[0]), onehot[:, 0:OWN])) - jnp.concatenate([centres[0]] * K, axis=1)]
                else:
                    middle = (OWN + EDGES) // 2
                    apart = [
                        joined(dot(thirds(ext), onehot[:, a:b])) - jnp.concatenate([centre] * (K // 2), axis=1)
                        for ext, centre, a, b in (
                            (exts[1], centres[1], OWN, middle), (exts[2], centres[2], middle, EDGES))
                    ]
                across = jnp.where(spatial, jnp.concatenate(apart, axis=1), 0.0)
                squared = jnp.broadcast_to(jnp.sum(across * across, axis=0, keepdims=True), (8, OWN)) + SOFTEN
                rd = lax.rsqrt(squared)
                rd = rd * (1.5 - 0.5 * squared * rd * rd)
                t = jnp.minimum(squared * rd * (1.0 / CUTOFF), 1.0)
                y = order * t
                turns = jnp.floor(y + 0.5)
                r = y - turns
                sign = 1.0 - 2.0 * (turns - 2.0 * jnp.floor(0.5 * turns))
                z = r * r
                sine = sign * r * polynomial(SIN_TERMS, z)
                cosine = sign * polynomial(COS_TERMS, z)
                t2 = t * t
                t4 = t2 * t2
                envelope = 1.0 + t4 * t * (-21.0 + t * (35.0 - 15.0 * t))
                fall = -105.0 * t4 * (1.0 - t) * (1.0 - t)
                front = math.sqrt(2.0 / CUTOFF) * rd
                bessel = front * sine * envelope
                slope = front * (
                    order * (math.pi / CUTOFF) * cosine * envelope + sine * (fall * (1.0 / CUTOFF) - envelope * rd))
                unit[:, begin:end] = across * rd
                inverse[:, begin:end] = rd
                hi = bessel.astype(BF16).astype(F32)
                hi_slope = slope.astype(BF16).astype(F32)
                bessels[:, begin:end] = jnp.concatenate(
                    [hi, bessel - hi, hi_slope, slope - hi_slope], axis=0).astype(BF16)

            for i in range(EDGES // CHUNK):
                here = slice(i * CHUNK, (i + 1) * CHUNK)
                if here.start < OWN:
                    pre = dot(basis_t[...], bessels[:, here])
                    grow = pre[128:256]
                    pre = pre[0:128]
                else:
                    pre = dot(basis_t[0:64, :], bessels[:, here])
                    grow = dot(basis_t[128:192, :], bessels[:, here])
                sg = sigmoid(pre)
                hidden = pre * sg
                hi, lo = halves(hidden)
                dhi, dlo = halves((sg + hidden * (1.0 - sg)) * grow)
                r1[:, here] = dot(out1_t[...], jnp.concatenate([hi[0:64], lo[0:64]], axis=0))
                r1d[:, here] = dot(out1_t[...], jnp.concatenate([dhi[0:64], dlo[0:64]], axis=0))
                if here.start < OWN:
                    r2[:, here] = dot(out2_t[...], jnp.concatenate([hi[64:128], lo[64:128]], axis=0))
                    r2d[:, here] = dot(out2_t[...], jnp.concatenate([dhi[64:128], dlo[64:128]], axis=0))

            def messages(cc, c):
                at = pl.multiple_of(cc * 32, 32)
                sums = []
                for first, last in SEGMENTS:
                    m = [jnp.zeros((32, A), F32) for _ in range(4)]
                    for b in range(first, last):
                        here = slice(b * A, (b + 1) * A)
                        sender = lift[pl.ds(at, 32), here]
                        m[0] = m[0] + r1[pl.ds(at, 32), here] * sender
                        through = r1[pl.ds(C + at, 32), here] * sender
                        for d in range(3):
                            m[1 + d] = m[1 + d] + unit[d:d + 1, here] * through
                    sums.append(m)
                for d in range(4):
                    row = pl.ds(d * C + at, 32)
                    nodes[row, 0:A] = sums[0][d]
                    lo, up = sums[1][d], sums[2][d]
                    lo = lo + pltpu.roll(lo, 64, 1)
                    up = up + pltpu.roll(up, 64, 1)
                    nodes[row, A:2 * A] = jnp.where(lanes_below_64((32, A)), lo, up)
                return c

            lax.fori_loop(0, C // 32, messages, 0, unroll=True)

            vectors = [nodes[(1 + d) * C:(2 + d) * C, :] for d in range(3)]
            squares = vectors[0] * vectors[0] + vectors[1] * vectors[1] + vectors[2] * vectors[2]
            scalars = h0[...] + mm2(blend1_t[...], jnp.concatenate([nodes[0:C, :], squares], axis=0))
            e1 = jnp.sum(head1_col[...] * scalars[:, 0:A], axis=0, keepdims=True)
            kept = [scalars.astype(BF16)] + [mm2(change1_t[...], v).astype(BF16) for v in vectors]
            projected = jnp.concatenate([dot(source2_t[...], f) for f in kept], axis=0)
            sv_hi, sv_lo = halves(projected)

            def gather2(i, c):
                hot = onehot[:, chunk_of(i)]
                sv[:, chunk_of(i)] = dot(sv_hi, hot) + dot(sv_lo, hot)
                return c

            lax.fori_loop(0, OWN // CHUNK, gather2, 0, unroll=True)

            def messages2(cc, c):
                at = pl.multiple_of(cc * 32, 32)
                total = jnp.zeros((32, A), F32)
                for b in range(K):
                    here = slice(b * A, (b + 1) * A)
                    along = unit[0:1, here] * sv[pl.ds(C + at, 32), here]
                    along = along + unit[1:2, here] * sv[pl.ds(2 * C + at, 32), here]
                    along = along + unit[2:3, here] * sv[pl.ds(3 * C + at, 32), here]
                    total = total + r2[pl.ds(at, 32), here] * sv[pl.ds(at, 32), here]
                    total = total + r2[pl.ds(C + at, 32), here] * along
                acc2[pl.ds(at, 32), :] = total
                return c

            lax.fori_loop(0, C // 32, messages2, 0, unroll=True)

            mixed = kept[0][:, 0:A].astype(F32) + mm2(blend2_t[...], acc2[...])
            pre = mm2(head2_t[...], mixed)
            sg = sigmoid(pre)
            hidden = pre * sg
            e2 = jnp.sum(proj2_col[...] * hidden, axis=0, keepdims=True)
            energy_row[...] = live * (e1 + e2)
            dpre = proj2_col[...] * live * (sg + hidden * (1.0 - sg))
            dmixed = mm2(head2_n[...], dpre)
            da2[...] = mm2(blend2_in[...], dmixed)

            du[...] = jnp.zeros((32, EDGES), F32)

            def backward2(cc, c):
                at = pl.multiple_of(cc * 32, 32)
                rows = [pl.ds(d * C + at, 32) for d in range(4)]
                da = da2[rows[0], :]
                for b in range(K):
                    here = slice(b * A, (b + 1) * A)
                    w0 = r2[rows[0], here]
                    through = da * r2[rows[1], here]
                    dsv[rows[0], here] = (da * w0).astype(BF16)
                    along = None
                    for d in range(3):
                        u = unit[d:d + 1, here]
                        v = sv[rows[1 + d], here]
                        along = u * v if along is None else along + u * v
                        dsv[rows[1 + d], here] = (u * through).astype(BF16)
                        du[8 * d:8 * d + 8, here] += octets(through * v)
                    du[24:32, here] += octets(da * (r2d[rows[0], here] * sv[rows[0], here] + r2d[rows[1], here] * along))
                return c

            lax.fori_loop(0, C // 32, backward2, 0, unroll=True)

            dproj = jnp.concatenate(
                [dot_nt(dsv[2 * C * q:2 * C * (q + 1)], onehot[:, 0:OWN]) for q in range(2)], axis=0)
            dkept = [mm2(source2_s[...], dproj[d * C:(d + 1) * C]) for d in range(4)]
            dscalars = dkept[0] + jnp.concatenate(
                [dmixed + head1_col[...] * live, jnp.zeros((C, A), F32)], axis=1)
            dx = mm2(blend1_in[...], dscalars)
            dm = [dx[0:C]]
            for d in range(3):
                dm.append(mm2(change1_in[...], dkept[1 + d]) + 2.0 * vectors[d] * dx[C:2 * C])
            for d in range(4):
                row = slice(d * C, (d + 1) * C)
                dnodes[row, 0:A] = dm[d][:, 0:A]
                dnodes[row, A:2 * A] = lower_twice(dm[d][:, A:])
                dnodes[row, 2 * A:3 * A] = upper_twice(dm[d][:, A:])

            def backward1(cc, c):
                at = pl.multiple_of(cc * 32, 32)
                rows = [pl.ds(d * C + at, 32) for d in range(4)]
                for s, (first, last) in enumerate(SEGMENTS):
                    g = [dnodes[rows[d], s * A:(s + 1) * A] for d in range(4)]
                    for b in range(first, last):
                        here = slice(b * A, (b + 1) * A)
                        sender = lift[rows[0], here]
                        through = r1[rows[1], here] * sender
                        along = None
                        for d in range(3):
                            u = unit[d:d + 1, here]
                            along = u * g[1 + d] if along is None else along + u * g[1 + d]
                            du[8 * d:8 * d + 8, here] += octets(through * g[1 + d])
                        du[24:32, here] += octets(sender * (g[0] * r1d[rows[0], here] + along * r1d[rows[1], here]))
                return c

            lax.fori_loop(0, C // 32, backward1, 0, unroll=True)

            for begin, end in ((0, OWN), (OWN, EDGES)):
                here = slice(begin, end)
                on_distance = jnp.sum(du[24:32, here], axis=0, keepdims=True)
                on_unit = jnp.zeros((8, OWN), F32)
                for d in range(3):
                    part = jnp.sum(du[8 * d:8 * d + 8, here], axis=0, keepdims=True)
                    on_unit = jnp.where(wide8 == d, part, on_unit)
                u = unit[:, here]
                rd = inverse[:, here]
                on_distance = on_distance - jnp.sum(u * on_unit, axis=0, keepdims=True) * rd
                dacross[:, here] = on_unit * rd + u * on_distance

            sums, spreads = [], []
            for first, last in SEGMENTS:
                total = dacross[:, first * A:(first + 1) * A]
                for b in range(first + 1, last):
                    total = total + dacross[:, b * A:(b + 1) * A]
                sums.append(total)
                here = slice(first * A, last * A)
                spreads.append(joined(dot_nt(thirds(dacross[:, here]), onehot[:, here])))
            xo, xl, xu = spreads
            lo = sums[1] + pltpu.roll(sums[1], 64, 1)
            up = sums[2] + pltpu.roll(sums[2], 64, 1)
            ghosts = xo[:, A:] - jnp.where(below, lo, up)
            b_out[it, 0, :, A:] = xl[:, A:]
            b_out[it, 0, :, :A] = jnp.zeros((8, A), F32)
            b_out[it, 1, :, :A] = xl[:, :A]
            b_out[it, 1, :, A:] = ghosts
            b_out[it, 2, :, :A] = xu[:, :A]
            b_out[it, 2, :, A:] = ghosts
            b_out[it, 3, :, A:] = xu[:, A:]
            b_out[it, 3, :, :A] = jnp.zeros((8, A), F32)
            o_out[:, 0:A] = xo[:, :A] - sums[0]
            o_out[:, A:2 * A] = jnp.where(below, xu[:, A:], xl[:, A:])
            for copy in b_copies(it):
                copy.start()

            @pl.when(it < EVALS - 1)
            def _():
                for copy in b_copies(it):
                    copy.wait()
                gradient = assembled([b_in[it, j] for j in range(4)], o_out[...], listhot[...])
                frc[...] = -gradient
                half[...] = half[...] - 0.5 * TIMESTEP * gradient * inertia
                advance(it + 1)
                for copy in a_copies(it + 1):
                    copy.start()

            return carry

        for it in range(EVALS):
            evaluate(it, 0)

        energy = jnp.broadcast_to(jnp.sum(energy_row[...], axis=1, keepdims=True), (8, A))
        o_out[:, 2 * A:3 * A] = jnp.where(rows8 == 3, energy, pos[...])
        o_out[:, 3 * A:4 * A] = half[...]
        for copy in c_copies():
            copy.start()
        lane = lax.broadcasted_iota(I32, (1, replicas), 1)
        level = levels_in[...]
        here = jnp.sum(jnp.where(lane == rep, level, 0.0), axis=1, keepdims=True)
        there = jnp.sum(
            jnp.where(lane == jnp.broadcast_to(target_in[...], (1, replicas)), level, 0.0), axis=1, keepdims=True)
        factor = jnp.broadcast_to(jnp.sqrt(here / there), (8, A))
        for copy in l_copies():
            copy.wait()

        def chosen(own, sent, shape):
            which = jnp.broadcast_to(target_in[...], shape)
            return jnp.where(which == rep - 1, sent[0], jnp.where(which == rep + 1, sent[1], own))

        columns = chosen(l_out[...], (l_in[0], l_in[1]), (8, A))
        hot = (numbers.astype(F32) == jnp.broadcast_to(columns[0:1], (A, A))).astype(F32).astype(BF16)
        for copy in b_copies(EVALS - 1) + c_copies():
            copy.wait()
        parts = [chosen(b_in[EVALS - 1, j], (c_in[0, j], c_in[1, j]), (8, 2 * A)) for j in range(4)]
        own = chosen(o_out[...], (o_in[0], o_in[1]), (8, 4 * A))
        gradient = assembled(parts, own, hot)
        first = own[:, 2 * A:3 * A]
        second = (own[:, 3 * A:4 * A] - 0.5 * TIMESTEP * gradient * inertia) * factor
        last = -gradient
        for d in range(3):
            pos_out[d] = first[d:d + 1]
            vel_out[d] = second[d:d + 1]
            frc_out[d] = last[d:d + 1]
        energy_out[...] = first[3:4, 0:1]

    return kernel


def solution(mesh):
    domains, replicas = mesh.shape["dom"], mesh.shape["rep"]

    def on_device(
        particle_locations, particle_speeds, acting_pulls, reciprocal_particle_inertia, particle_elements,
        domain_real_particles, halo_send_places, adjacency_places, filled_adjacency_places, exchange_target,
        thermal_levels, element_features, first_distance_expansion, first_distance_filter, first_source_projection,
        first_invariant_blend, first_directional_change, first_linear_potential_head, second_distance_expansion,
        second_distance_filter, second_source_projection, second_invariant_blend, final_head_intermediate,
        final_head_projection,
    ):
        f32 = lambda *shape: pltpu.VMEM(shape, F32)
        bf16 = lambda *shape: pltpu.VMEM(shape, BF16)
        dma = lambda *shape: pltpu.SemaphoreType.DMA(shape)
        scratch = [
            f32(8, A), f32(8, A), f32(8, A), f32(2 * K, A), bf16(2 * A, EDGES), bf16(A, A), f32(C, EDGES),
            f32(C, 2 * A), f32(C, C),
            bf16(C, 2 * C), bf16(C, C), bf16(C, C), bf16(C, C), bf16(C, C), bf16(C, 16), bf16(256, 32),
            bf16(2 * C, 128), bf16(2 * C, 128), f32(C, A), f32(16, A),
            f32(8, EDGES), f32(8, EDGES), bf16(32, EDGES), f32(2 * C, EDGES), f32(2 * C, EDGES),
            f32(2 * C, OWN), f32(2 * C, OWN), f32(4 * C, OWN), f32(4 * C, 2 * A), f32(C, A), f32(C, A),
            bf16(4 * C, OWN), f32(32, EDGES), f32(4 * C, 3 * A), f32(8, EDGES), f32(1, A),
            f32(2, 8, 2 * A), f32(2, 4, 8, 2 * A), f32(K, A), f32(2, K, A), f32(2, 4, 8, 2 * A), f32(2, 4, 8, 2 * A),
            f32(2, 4, 8, 2 * A), f32(8, A), f32(2, 8, A), f32(8, 4 * A), f32(2, 8, 4 * A),
            dma(2, 4), dma(2, 4), dma(2), dma(2), dma(2, 4), dma(2, 4), dma(2, 4), dma(2, 4),
            dma(2), dma(2), dma(2), dma(2),
        ]
        vmem = pl.BlockSpec(memory_space=pltpu.VMEM)
        rowwise = lambda x: jnp.transpose(x, (1, 0, 2))
        outs = pl.pallas_call(
            make_kernel(domains, replicas),
            out_shape=[jax.ShapeDtypeStruct((3, 1, A), F32)] * 3 + [jax.ShapeDtypeStruct((1, 1), F32)],
            in_specs=[vmem] * 24,
            out_specs=[vmem] * 4,
            scratch_shapes=scratch,
            compiler_params=pltpu.CompilerParams(
                collective_id=0, has_side_effects=True, vmem_limit_bytes=56 * 1024 * 1024),
        )(
            rowwise(particle_locations), rowwise(particle_speeds), rowwise(acting_pulls),
            reciprocal_particle_inertia.reshape(1, A),
            particle_elements.reshape(1, A), domain_real_particles, halo_send_places, adjacency_places,
            filled_adjacency_places, exchange_target.reshape(1, 1), thermal_levels.reshape(1, -1),
            element_features, first_distance_expansion, first_distance_filter, first_source_projection,
            first_invariant_blend, first_directional_change, first_linear_potential_head.reshape(1, C),
            second_distance_expansion, second_distance_filter, second_source_projection, second_invariant_blend,
            final_head_intermediate.T, final_head_projection.reshape(1, -1),
        )
        return tuple(rowwise(x) for x in outs[:3]) + (outs[3],)

    split3, split2 = P("rep", None, "dom"), P("rep", "dom")
    return jax.shard_map(
        on_device, mesh=mesh,
        in_specs=(split3, split3, split3, P("dom"), P("dom"), split2, split3, split3, split2, P("rep")) + (P(),) * 14,
        out_specs=(split3, split3, split3, split2), check_vma=False)
```
